32 devices in a mesh: lsec: 8 (over z, x), rsec: 4 (over y, core).
Axes of the slice: x: 2, y: 2, z: 4, core: 2. Of those that a mesh axis runs over, the one named last changes fastest.
Arguments:
- psi: bfloat16 [2048, 1024], P('lsec', 'rsec'), may hold values from -8 to 8
- left_env: bfloat16 [12, 2048, 256], P(None, ('lsec', 'rsec')), may hold values from -2 to 2
- right_env: bfloat16 [12, 1024, 256], P(None, 'rsec', 'lsec'), may hold values from -2 to 2
- left_dims: int32 [8], P('lsec'), may hold values from 1 to 256, 1536 in all
- right_dims: int32 [4], P('rsec'), may hold values from 1 to 256, 768 in all
- term_shift: int32 [12, 2], replicated, may hold values from -1 to 1, as said below
Outputs:
- image_one: bfloat16 [2048, 1024], P('lsec', 'rsec')
- image_two: bfloat16 [2048, 1024], P('lsec', 'rsec')
- projected: float32 [2, 2], replicated
The draws below stay inside these ranges and needn't reach their ends.
Inputs may be any that keep to these rules, and one draw needn't show every extreme that they name: `term_shift`: each term shifts the left and the right sector by -1, 0 or 1; each of the nine pairs of shifts belongs to some term.
All inputs are finite; a program needn't handle non-finite values. No bound on the sum of `left_dims` or of `right_dims` on one device may be relied on, other than what follows from the above.
Results may differ from the reference program's by a relative error of at most 0.0095.
Values may be sent and summed in bfloat16 or wider, within the bound.
A program may use at most 64 MiB of HBM per device.

```python
import math
import jax
import jax.numpy as jnp
import numpy as np
from jax import lax

DB = 256
W = 12
NL = 8
NR = 4


def draw_term_shift(key, part):
    order = jax.random.permutation(key, W)
    combo = order % 9
    return jnp.stack([combo // 3 - 1, combo % 3 - 1], axis=1).astype(jnp.int32)


def draw_psi(key, part):
    rows = jnp.arange(NL * DB, dtype=jnp.float32) / float(NL * DB - 1)
    base = jnp.clip(jax.random.normal(key, (NL * DB, NR * DB), jnp.float32), -4.0, 4.0)
    amp = jnp.exp(rows * jnp.log(2.0))[:, None] * jnp.ones((1, NR * DB), jnp.float32)
    return (base * amp).astype(jnp.bfloat16)


def env_blocks(key, sectors):
    shape = (W, sectors * DB, DB)
    noise = jnp.clip(jax.random.normal(key, shape, jnp.float32), -4.0, 4.0)
    rows = jnp.arange(sectors * DB, dtype=jnp.int32) % DB
    cols = jnp.arange(DB, dtype=jnp.int32)
    diagonal = (rows[:, None] == cols[None, :]).astype(jnp.float32)
    return (noise * float(DB) ** (-0.5) + diagonal[None, :, :]).astype(jnp.bfloat16)


def draw_left_env(key, part):
    return env_blocks(jax.random.fold_in(key, 11), NL)


def draw_right_env(key, part):
    return env_blocks(jax.random.fold_in(key, 23), NR)


def length_profile(amount, total, most, slope):
    weights = [(1 << 20) // math.isqrt(standing ** slope) + 1 for standing in range(2, amount + 1)]
    spare, counts = total - most - (amount - 1), [1] * (amount - 1)
    while spare > 0:
        free = [i for i in range(amount - 1) if counts[i] < most]
        mass, left = sum([weights[i] for i in free]), spare
        for i in free:
            extra = min(most - counts[i], max(1, left * weights[i] // mass), spare)
            counts[i] = counts[i] + extra
            spare = spare - extra
    return np.array([most] + counts)


def uneven_parts(stream_key, number_of, total, most, slope):
    if number_of == 2:
        one = jax.random.randint(stream_key, (), max(1, total - most), min(most, total - 1) + 1)
        return jnp.stack([one, total - one])
    lengths = jnp.asarray(length_profile(number_of, total, most, slope), jnp.int32)
    pairs = (number_of - 1) // 2
    donor, receiver = lengths[1:1 + 2 * pairs:2], lengths[2:2 + 2 * pairs:2]
    room = jnp.minimum(donor - 1, most - receiver)
    moved = jax.random.randint(jax.random.fold_in(stream_key, 1), (pairs,), 0, 1 << 20) % (room + 1)
    lengths = lengths.at[1:1 + 2 * pairs:2].set(donor - moved).at[2:2 + 2 * pairs:2].set(receiver + moved)
    return lengths[jax.random.permutation(jax.random.fold_in(stream_key, 2), number_of)]


def setup_inputs(seed: int = 0) -> dict:
    seeds = jax.random.split(jax.random.key(seed), 7)
    return {
        "psi": draw_psi(jax.random.fold_in(seeds[6], 71), 0),
        "left_env": draw_left_env(jax.random.fold_in(seeds[6], 71), 0),
        "right_env": draw_right_env(jax.random.fold_in(seeds[6], 71), 0),
        "left_dims": uneven_parts(seeds[3], NL, NL * DB * 3 // 4, DB, 2).astype(jnp.int32),
        "right_dims": uneven_parts(seeds[4], NR, NR * DB * 3 // 4, DB, 2).astype(jnp.int32),
        "term_shift": draw_term_shift(jax.random.fold_in(seeds[6], 71), 0),
    }


def live_mask(left_dims, right_dims):
    rows = jnp.arange(NL * DB, dtype=jnp.int32)
    cols = jnp.arange(NR * DB, dtype=jnp.int32)
    row_live = rows % DB < left_dims[rows // DB]
    col_live = cols % DB < right_dims[cols // DB]
    return row_live[:, None] & col_live[None, :]

def apply_terms(vector, left_env, right_env, term_shift, mask):
    blocks = vector.reshape(NL, DB, NR, DB)
    padded = jnp.pad(blocks, ((1, 1), (0, 0), (1, 1), (0, 0)))
    total = jnp.zeros((NL, DB, NR, DB), jnp.float32)
    zero = jnp.zeros((), jnp.int32)
    for term in range(W):
        start_left = (1 - term_shift[term, 0]).astype(jnp.int32)
        start_right = (1 - term_shift[term, 1]).astype(jnp.int32)
        source = lax.dynamic_slice(padded, (start_left, zero, start_right, zero), (NL, DB, NR, DB))
        left_blocks = left_env[term].reshape(NL, DB, DB).astype(jnp.float32)
        inner = jnp.einsum('aik,akbj->aibj', left_blocks, source.astype(jnp.float32)).astype(jnp.bfloat16)
        inner = lax.optimization_barrier(inner)
        right_blocks = right_env[term].reshape(NR, DB, DB).astype(jnp.float32)
        total = total + jnp.einsum('aibj,bjn->aibn', inner.astype(jnp.float32), right_blocks)
    return total.reshape(NL * DB, NR * DB) * mask.astype(jnp.float32)

def reference(psi, left_env, right_env, left_dims, right_dims, term_shift):
    mask = live_mask(left_dims, right_dims)
    live = jnp.where(mask, psi, jnp.zeros_like(psi))
    count = float(NL * NR * DB * DB)
    live32 = live.astype(jnp.float32)
    total_sq = jnp.sum(live32 * live32)
    first = (live32 * lax.rsqrt(total_sq / count + 1e-06)).astype(jnp.bfloat16)
    image1 = apply_terms(first, left_env, right_env, term_shift, mask)
    first32 = first.astype(jnp.float32)
    alpha = jnp.sum(first32 * image1) / count
    rest = image1 - alpha * first32
    rest_sq = jnp.sum(rest * rest) / count
    second = (rest * lax.rsqrt(rest_sq + 1e-06)).astype(jnp.bfloat16)
    image2 = apply_terms(second, left_env, right_env, term_shift, mask)
    second32 = second.astype(jnp.float32)
    upper = jnp.sum(first32 * image2) / count
    lower = jnp.sum(second32 * image1) / count
    corner = jnp.sum(second32 * image2) / count
    projected = jnp.stack([jnp.stack([alpha, upper]), jnp.stack([lower, corner])])
    return (image1.astype(jnp.bfloat16), image2.astype(jnp.bfloat16), projected)
```

```python
import functools

import jax
import jax.numpy as jnp
from jax import lax
from jax.experimental import pallas as pl
from jax.experimental.pallas import tpu as pltpu
from jax.sharding import PartitionSpec as P

MESH = pl.DeviceIdType.MESH
F32 = jnp.float32
BF16 = jnp.bfloat16
NT = (((1,), (1,)), ((), ()))
NN = (((1,), (0,)), ((), ()))


def kernel(
    nl, nr, gather_right, terms,
    shift_ref, ldim_ref, rdim_ref, psi_ref, left_ref, right_ref,
    image1_ref, image2_ref, proj_ref,
    live, first, images, inner, lbuf, rbuf, w1_ref, part, row_sum, row_slots, col_slots,
    l_send, l_recv, r_send, r_recv, h_send, h_recv, ar_send, ar_recv, ac_send, ac_recv,
):
    width = psi_ref.shape[0]
    count = float(nl * nr * width * width)
    li, ri = lax.axis_index("lsec"), lax.axis_index("rsec")
    pending = []

    def when(cond, fn):
        if cond is None:
            fn()
        else:
            pl.when(cond)(fn)

    def send(src, dst, send_sem, recv_sem, device, cond=None):
        copy = pltpu.make_async_remote_copy(
            src_ref=src, dst_ref=dst, send_sem=send_sem, recv_sem=recv_sem,
            device_id=device, device_id_type=MESH,
        )
        when(cond, copy.start)
        pending.append((copy, cond))

    def arrive(dst, send_sem, recv_sem, device, cond=None):
        copy = pltpu.make_async_remote_copy(
            src_ref=dst, dst_ref=dst, send_sem=send_sem, recv_sem=recv_sem,
            device_id=device, device_id_type=MESH,
        )
        when(cond, copy.wait_recv)

    barrier = pltpu.get_barrier_semaphore()

    def greet_col(i, _):
        pl.semaphore_signal(
            barrier, inc=1, device_id=(lax.rem(li + i, nl), ri), device_id_type=MESH
        )
        return 0

    def greet_row(i, _):
        pl.semaphore_signal(
            barrier, inc=1, device_id=(li, lax.rem(ri + i, nr)), device_id_type=MESH
        )
        return 0

    lax.fori_loop(1, nl, greet_col, 0)
    lax.fori_loop(1, nr, greet_row, 0)

    rows = lax.broadcasted_iota(jnp.int32, (width, width), 0)
    cols = lax.broadcasted_iota(jnp.int32, (width, width), 1)
    mask = ((rows < ldim_ref[0]) & (cols < rdim_ref[0])).astype(F32)

    def lanes(x):
        total = jnp.sum(x, axis=0, keepdims=True)
        out = total[:, 0:128]
        for at in range(128, width, 128):
            out = out + total[:, at:at + 128]
        return out

    live32 = psi_ref[...].astype(F32) * mask
    live[4] = live32.astype(BF16)
    part[...] = jnp.zeros_like(part)
    part[0, 0:1, :] = lanes(live32 * live32)

    lbuf[pl.ds(ri, 1)] = left_ref[...][None]
    if gather_right:
        ncol = right_ref.shape[1]
        eye = (
            lax.broadcasted_iota(jnp.int32, (ncol, ncol), 0)
            == lax.broadcasted_iota(jnp.int32, (ncol, ncol), 1)
        ).astype(BF16)
        turned = lax.dot_general(
            eye, right_ref[...], NT, preferred_element_type=F32
        ).astype(BF16)
        for w in range(terms):
            rbuf[pl.ds(li, 1), w * ncol:(w + 1) * ncol, :] = turned[
                :, w * width:(w + 1) * width
            ][None]

    for store in (live, images):
        for k in range(9):
            dl, dr = k // 3 - 1, k % 3 - 1
            outside = (li - dl < 0) | (li - dl >= nl) | (ri - dr < 0) | (ri - dr >= nr)
            if k != 4:
                def clear(store=store, k=k):
                    store[k] = jnp.zeros((width, width), BF16)
                pl.when(outside)(clear)

    pl.semaphore_wait(barrier, nl + nr - 2)

    def reduce_start(t):
        for i in range(1, nr):
            other = lax.rem(ri + i, nr)
            send(part.at[t], row_slots.at[t, ri], ar_send.at[t, i], ar_recv.at[t, ri], (li, other))

    def reduce_middle(t):
        for i in range(1, nr):
            other = lax.rem(ri + i, nr)
            arrive(row_slots.at[t, other], ar_send.at[t, i], ar_recv.at[t, other], (li, other))
        row_slots[t, pl.ds(ri, 1)] = part[t][None]
        total = row_slots[t, 0]
        for i in range(1, nr):
            total = total + row_slots[t, i]
        row_sum[t] = total
        for i in range(1, nl):
            other = lax.rem(li + i, nl)
            send(row_sum.at[t], col_slots.at[t, li], ac_send.at[t, i], ac_recv.at[t, li], (other, ri))

    def reduce_end(t):
        for i in range(1, nl):
            other = lax.rem(li + i, nl)
            arrive(col_slots.at[t, other], ac_send.at[t, i], ac_recv.at[t, other], (other, ri))
        col_slots[t, pl.ds(li, 1)] = row_sum[t][None]
        total = col_slots[t, 0]
        for i in range(1, nl):
            total = total + col_slots[t, i]
        return jnp.sum(total, axis=1, keepdims=True)

    def gather(buf, n, me, device, send_sem, recv_sem):
        inner_n = 2
        outer = n // inner_n
        o, i = me // inner_n, lax.rem(me, inner_n)
        pair = me + 1 - 2 * i
        pair_dev = device(pair)

        def forward(slot, cond=None):
            at = slot * inner_n + i
            send(buf.at[at], buf.at[at], send_sem.at[2, slot], recv_sem.at[at], pair_dev, cond)

        forward(o)
        for s in range(outer - 1):
            low, high = o - s, o + s
            at = jnp.maximum(low, 0) * inner_n + i
            send(
                buf.at[at], buf.at[at], send_sem.at[0, s], recv_sem.at[at],
                device(jnp.minimum(me + inner_n, n - 1)), (low >= 0) & (o < outer - 1),
            )
            at = jnp.minimum(high, outer - 1) * inner_n + i
            send(
                buf.at[at], buf.at[at], send_sem.at[1, s], recv_sem.at[at],
                device(jnp.maximum(me - inner_n, 0)), (high < outer) & (o > 0),
            )
            yield
            for got, cond in ((low - 1, low - 1 >= 0), (high + 1, high + 1 < outer)):
                got = jnp.clip(got, 0, outer - 1)
                at = got * inner_n + i
                arrive(buf.at[at], send_sem.at[0, s], recv_sem.at[at], pair_dev, cond)
                forward(got, cond)
        yield
        for slot in range(outer):
            at = slot * inner_n + 1 - i
            arrive(buf.at[at], send_sem.at[2, slot], recv_sem.at[at], pair_dev)

    def halo(buf, t):
        up, down = (jnp.minimum(li + 1, nl - 1), ri), (jnp.maximum(li - 1, 0), ri)
        east, west = (li, jnp.minimum(ri + 1, nr - 1)), (li, jnp.maximum(ri - 1, 0))

        def sideways(k, cond):
            go = ri < nr - 1
            send(buf.at[k], buf.at[k + 1], h_send.at[t, k + 1], h_recv.at[t, k + 1], east,
                 go if cond is None else go & cond)
            go = ri > 0
            send(buf.at[k], buf.at[k - 1], h_send.at[t, k - 1], h_recv.at[t, k - 1], west,
                 go if cond is None else go & cond)

        send(buf.at[4], buf.at[7], h_send.at[t, 7], h_recv.at[t, 7], up, li < nl - 1)
        send(buf.at[4], buf.at[1], h_send.at[t, 1], h_recv.at[t, 1], down, li > 0)
        sideways(4, None)
        yield
        for k, cond in ((7, li > 0), (1, li < nl - 1)):
            arrive(buf.at[k], h_send.at[t, k], h_recv.at[t, k], up, cond)
            sideways(k, cond)
        yield
        for k, l_ok in ((4, None), (7, li > 0), (1, li < nl - 1)):
            for at, r_ok in ((k + 1, ri > 0), (k - 1, ri < nr - 1)):
                arrive(buf.at[at], h_send.at[t, at], h_recv.at[t, at], up,
                       r_ok if l_ok is None else r_ok & l_ok)

    def apply_left(vec):
        for w in range(terms):
            k = (shift_ref[w, 0] + 1) * 3 + shift_ref[w, 1] + 1
            mine = lbuf.shape[1] // terms
            a = lbuf[:, w * mine:(w + 1) * mine, :].reshape(width, width)
            product = jnp.dot(a, vec[k], preferred_element_type=F32)
            inner[w] = product.astype(BF16)

    def apply_right():
        total = jnp.zeros((width, width), F32)
        for w in range(terms):
            if gather_right:
                b = rbuf[:, w * ncol:(w + 1) * ncol, :].reshape(width, width)
                total = total + lax.dot_general(inner[w], b, NT, preferred_element_type=F32)
            else:
                total = total + lax.dot_general(
                    inner[w], right_ref[w], NN, preferred_element_type=F32
                )
        return total * mask

    reduce_start(0)
    halo1 = halo(live, 0)
    next(halo1)
    gathers = [gather(lbuf, nr, ri, lambda r: (li, r), l_send, l_recv)]
    if gather_right:
        gathers.append(gather(rbuf, nl, li, lambda l: (l, ri), r_send, r_recv))
    for g in gathers:
        next(g)
    reduce_middle(0)
    next(halo1)
    steps = [nr // 2 - 1, nl // 2 - 1][:len(gathers)]
    for s in range(max(steps)):
        for g, n in zip(gathers, steps):
            if s < n:
                next(g)
    for _ in halo1:
        pass
    ss = reduce_end(0)[0:1]
    scale = lax.rsqrt(ss / count + 1e-06)
    for k in range(9):
        first[k] = (live[k].astype(F32) * scale).astype(BF16)
    for _ in gathers[0]:
        pass
    apply_left(first)
    for g in gathers[1:]:
        for _ in g:
            pass
    w1 = apply_right()
    w1_bf16 = w1.astype(BF16)
    images[4] = w1_bf16
    halo2 = halo(images, 1)
    next(halo2)
    image1_ref[...] = w1_bf16
    w1_ref[...] = w1
    v1 = first[4].astype(F32)
    part[1, 0:1, :] = lanes(v1 * w1)
    part[1, 1:2, :] = lanes(w1 * w1)
    part[1, 2:3, :] = lanes(v1 * v1)
    reduce_start(1)
    next(halo2)
    reduce_middle(1)
    for _ in halo2:
        pass
    apply_left(images)
    sums = reduce_end(1)
    alpha = sums[0:1] / count
    nr_ = sums[1:2] / count - 2.0 * alpha * alpha + alpha * alpha * (sums[2:3] / count)
    factor = lax.rsqrt(jnp.maximum(nr_, 0.0) + 1e-06)
    w1 = w1_ref[...]
    w2 = (apply_right() - alpha * w1) * factor
    v1 = first[4].astype(F32)
    v2 = ((w1 - alpha * v1) * factor).astype(BF16).astype(F32)
    part[2, 0:1, :] = lanes(v1 * w2)
    part[2, 1:2, :] = lanes(v2 * w1)
    part[2, 2:3, :] = lanes(v2 * w2)
    reduce_start(2)
    image2_ref[...] = w2.astype(BF16)
    reduce_middle(2)
    sums = reduce_end(2) / count
    r8 = lax.broadcasted_iota(jnp.int32, (8, 128), 0)
    c8 = lax.broadcasted_iota(jnp.int32, (8, 128), 1)
    top = jnp.where(c8 == 0, alpha, sums[0:1])
    bottom = jnp.where(c8 == 0, sums[1:2], sums[2:3])
    proj_ref[...] = jnp.where(r8 == 0, top, bottom)

    for copy, cond in pending:
        when(cond, copy.wait_send)


def on_device(nl, nr, psi, left_env, right_env, left_dims, right_dims, term_shift):
    width = psi.shape[0]
    terms = left_env.shape[0]
    mine = left_env.shape[1]
    ncol = right_env.shape[2]
    gather_right = ncol % 16 == 0
    left = left_env.reshape(terms * mine, width)
    if gather_right:
        right = right_env.reshape(terms * width, ncol)
        rshape = (nl, terms * ncol, width)
    else:
        right = lax.all_gather(right_env, "lsec", axis=2, tiled=True)
        rshape = (1, 16, 128)
    vmem = pl.BlockSpec(memory_space=pltpu.VMEM)
    smem = pl.BlockSpec(memory_space=pltpu.SMEM)
    dma = pltpu.SemaphoreType.DMA
    image1, image2, proj = pl.pallas_call(
        functools.partial(kernel, nl, nr, gather_right, terms),
        out_shape=(
            jax.ShapeDtypeStruct((width, width), BF16),
            jax.ShapeDtypeStruct((width, width), BF16),
            jax.ShapeDtypeStruct((8, 128), F32),
        ),
        in_specs=[smem] * 3 + [vmem] * 3,
        out_specs=(vmem, vmem, vmem),
        scratch_shapes=[
            pltpu.VMEM((9, width, width), BF16),
            pltpu.VMEM((9, width, width), BF16),
            pltpu.VMEM((9, width, width), BF16),
            pltpu.VMEM((terms, width, width), BF16),
            pltpu.VMEM((nr, terms * mine, width), BF16),
            pltpu.VMEM(rshape, BF16),
            pltpu.VMEM((width, width), F32),
            pltpu.VMEM((3, 8, 128), F32),
            pltpu.VMEM((3, 8, 128), F32),
            pltpu.VMEM((3, nr, 8, 128), F32),
            pltpu.VMEM((3, nl, 8, 128), F32),
            dma((3, nr)),
            dma((nr,)),
            dma((3, nl)),
            dma((nl,)),
            dma((2, 9)),
            dma((2, 9)),
            dma((3, nr)),
            dma((3, nr)),
            dma((3, nl)),
            dma((3, nl)),
        ],
        compiler_params=pltpu.CompilerParams(
            collective_id=0, has_side_effects=True, vmem_limit_bytes=40 * 1024 * 1024
        ),
        cost_estimate=pl.CostEstimate(
            flops=8 * terms * width**3, bytes_accessed=4 * 2**20, transcendentals=2
        ),
    )(term_shift, left_dims, right_dims, psi, left, right)
    return image1, image2, proj[:2, :2]


def solution(mesh):
    nl, nr = mesh.shape["lsec"], mesh.shape["rsec"]
    in_specs = (
        P("lsec", "rsec"),
        P(None, ("lsec", "rsec"), None),
        P(None, "rsec", "lsec"),
        P("lsec"),
        P("rsec"),
        P(),
    )
    out_specs = (P("lsec", "rsec"), P("lsec", "rsec"), P())
    return jax.shard_map(
        functools.partial(on_device, nl, nr),
        mesh=mesh, in_specs=in_specs, out_specs=out_specs, check_vma=False,
    )
```

```python
import functools

import jax
import jax.numpy as jnp
from jax import lax
from jax.experimental import pallas as pl
from jax.experimental.pallas import tpu as pltpu
from jax.sharding import PartitionSpec as P

MESH = pl.DeviceIdType.MESH
F32 = jnp.float32
BF16 = jnp.bfloat16
NT = (((1,), (1,)), ((), ()))
NN = (((1,), (0,)), ((), ()))


def kernel(
    nl, nr, gather_right, terms,
    shift_ref, ldim_ref, rdim_ref, psi_ref, left_ref, right_ref,
    image1_ref, image2_ref, proj_ref,
    live, first, images, inner, lbuf, rbuf, w1_ref, part, row_sum, row_slots, col_slots,
    l_send, l_recv, r_send, r_recv, h_send, h_recv, ar_send, ar_recv, ac_send, ac_recv,
):
    width = psi_ref.shape[0]
    count = float(nl * nr * width * width)
    li, ri = lax.axis_index("lsec"), lax.axis_index("rsec")
    pending = []

    def when(cond, fn):
        if cond is None:
            fn()
        else:
            pl.when(cond)(fn)

    def send(src, dst, send_sem, recv_sem, device, cond=None):
        copy = pltpu.make_async_remote_copy(
            src_ref=src, dst_ref=dst, send_sem=send_sem, recv_sem=recv_sem,
            device_id=device, device_id_type=MESH,
        )
        when(cond, copy.start)
        pending.append((copy, cond))

    def arrive(dst, send_sem, recv_sem, device, cond=None):
        copy = pltpu.make_async_remote_copy(
            src_ref=dst, dst_ref=dst, send_sem=send_sem, recv_sem=recv_sem,
            device_id=device, device_id_type=MESH,
        )
        when(cond, copy.wait_recv)

    barrier = pltpu.get_barrier_semaphore()

    def greet_col(i, _):
        pl.semaphore_signal(
            barrier, inc=1, device_id=(lax.rem(li + i, nl), ri), device_id_type=MESH
        )
        return 0

    def greet_row(i, _):
        pl.semaphore_signal(
            barrier, inc=1, device_id=(li, lax.rem(ri + i, nr)), device_id_type=MESH
        )
        return 0

    lax.fori_loop(1, nl, greet_col, 0)
    lax.fori_loop(1, nr, greet_row, 0)

    rows = lax.broadcasted_iota(jnp.int32, (width, width), 0)
    cols = lax.broadcasted_iota(jnp.int32, (width, width), 1)
    mask = ((rows < ldim_ref[0]) & (cols < rdim_ref[0])).astype(F32)

    def lanes(x):
        total = jnp.sum(x, axis=0, keepdims=True)
        out = total[:, 0:128]
        for at in range(128, width, 128):
            out = out + total[:, at:at + 128]
        return out

    live32 = psi_ref[...].astype(F32) * mask
    live[4] = live32.astype(BF16)
    part[...] = jnp.zeros_like(part)
    part[0, 0:1, :] = lanes(live32 * live32)

    lbuf[pl.ds(ri, 1)] = left_ref[...][None]
    if gather_right:
        ncol = right_ref.shape[0] // terms
        rbuf[pl.ds(li, 1)] = right_ref[...][None]

    for store in (live, images):
        for k in range(9):
            dl, dr = k // 3 - 1, k % 3 - 1
            outside = (li - dl < 0) | (li - dl >= nl) | (ri - dr < 0) | (ri - dr >= nr)
            if k != 4:
                def clear(store=store, k=k):
                    store[k] = jnp.zeros((width, width), BF16)
                pl.when(outside)(clear)

    pl.semaphore_wait(barrier, nl + nr - 2)

    def reduce_start(t):
        for i in range(1, nr):
            other = lax.rem(ri + i, nr)
            send(part.at[t], row_slots.at[t, ri], ar_send.at[t, i], ar_recv.at[t, ri], (li, other))

    def reduce_middle(t):
        for i in range(1, nr):
            other = lax.rem(ri + i, nr)
            arrive(row_slots.at[t, other], ar_send.at[t, i], ar_recv.at[t, other], (li, other))
        row_slots[t, pl.ds(ri, 1)] = part[t][None]
        total = row_slots[t, 0]
        for i in range(1, nr):
            total = total + row_slots[t, i]
        row_sum[t] = total
        for i in range(1, nl):
            other = lax.rem(li + i, nl)
            send(row_sum.at[t], col_slots.at[t, li], ac_send.at[t, i], ac_recv.at[t, li], (other, ri))

    def reduce_end(t):
        for i in range(1, nl):
            other = lax.rem(li + i, nl)
            arrive(col_slots.at[t, other], ac_send.at[t, i], ac_recv.at[t, other], (other, ri))
        col_slots[t, pl.ds(li, 1)] = row_sum[t][None]
        total = col_slots[t, 0]
        for i in range(1, nl):
            total = total + col_slots[t, i]
        return jnp.sum(total, axis=1, keepdims=True)

    def gather(buf, n, me, device, send_sem, recv_sem, balance):
        outer = n // 2
        o, i = me // 2, lax.rem(me, 2)
        pair = me + 1 - 2 * i
        pair_dev = device(pair)
        balance = balance and outer > 2 and outer % 2 == 0
        mate = o + 1 - 2 * lax.rem(o, 2)
        half = buf.shape[1] // 2

        def piece(at, h):
            return buf.at[at, pl.ds(h * half, half)]

        def put(at, h, sem, dev, cond):
            send(piece(at, h), piece(at, h), sem, recv_sem.at[h, at], dev, cond)

        def got(at, h, cond=None):
            arrive(piece(at, h), send_sem.at[2, h, 0], recv_sem.at[h, at], pair_dev, cond)

        def forward(slot, h, cond=None):
            if balance and h == 1:
                cond = (slot != mate) if cond is None else cond & (slot != mate)
            put(slot * 2 + i, h, send_sem.at[2, h, slot], pair_dev, cond)

        for h in range(2):
            forward(o, h)
        for s in range(outer - 1):
            low, high = o - s, o + s
            up = device(jnp.minimum(me + 2, n - 1))
            down = device(jnp.maximum(me - 2, 0))
            for h in range(2):
                put(jnp.maximum(low, 0) * 2 + i, h, send_sem.at[0, h, s], up,
                    (low >= 0) & (o < outer - 1))
                put(jnp.minimum(high, outer - 1) * 2 + i, h, send_sem.at[1, h, s], down,
                    (high < outer) & (o > 0))
            if balance and s == 1:
                got(o * 2 + 1 - i, 1)
                put(o * 2 + 1 - i, 1, send_sem.at[3, 0, 0], device(mate * 2 + i), None)
            yield
            for h in range(2):
                for slot, cond in ((low - 1, low - 1 >= 0), (high + 1, high + 1 < outer)):
                    slot = jnp.clip(slot, 0, outer - 1)
                    got(slot * 2 + i, h, cond)
                    forward(slot, h, cond)
        yield
        for slot in range(outer):
            for h in range(2):
                early = balance and h == 1
                got(slot * 2 + 1 - i, h, (slot != o) if early else None)

    def halo(buf, t):
        outer = nl // 2
        o, i = li // 2, lax.rem(li, 2)
        from_pair, from_line = 1 + 6 * i, 7 - 6 * i
        pair = (li + 1 - 2 * i, ri)
        onward = (jnp.clip(li + 2 - 4 * i, 0, nl - 1), ri)
        goes = ((i == 0) & (o < outer - 1)) | ((i == 1) & (o > 0))
        comes = ((i == 0) & (o > 0)) | ((i == 1) & (o < outer - 1))
        east, west = (li, jnp.minimum(ri + 1, nr - 1)), (li, jnp.maximum(ri - 1, 0))
        half = width // 2

        def piece(k, c):
            return buf.at[k, pl.ds(c * half, half)]

        def put(src, dst, c, sem, dev, cond=None):
            send(piece(src, c), piece(dst, c), h_send.at[t, c, sem], h_recv.at[t, c, dst], dev, cond)

        def got(k, c, cond=None):
            arrive(piece(k, c), h_send.at[t, c, k], h_recv.at[t, c, k], pair, cond)

        def sideways(k, c, cond):
            go = ri < nr - 1
            put(k, k + 1, c, k + 1, east, go if cond is None else go & cond)
            go = ri > 0
            put(k, k - 1, c, k - 1, west, go if cond is None else go & cond)

        for c in range(2):
            put(4, from_line, c, 4, pair)
            sideways(4, c, None)
            yield
        for c in range(2):
            got(from_pair, c)
            put(from_pair, from_line, c, from_pair, onward, goes)
            sideways(from_pair, c, None)
        yield
        for c in range(2):
            got(from_line, c, comes)
            sideways(from_line, c, comes)
        yield
        for c in range(2):
            for k, l_ok in ((4, None), (from_pair, None), (from_line, comes)):
                for at, r_ok in ((k + 1, ri > 0), (k - 1, ri < nr - 1)):
                    got(at, c, r_ok if l_ok is None else r_ok & l_ok)

    def apply_left(vec):
        for w in range(terms):
            k = (shift_ref[0, w] + 1) * 3 + shift_ref[1, w] + 1
            mine = lbuf.shape[1] // terms
            a = lbuf[:, w * mine:(w + 1) * mine, :].reshape(width, width)
            product = jnp.dot(a, vec[k], preferred_element_type=F32)
            inner[w] = product.astype(BF16)

    def apply_right(c):
        half = width // 2
        at = slice(c * half, (c + 1) * half)
        total = jnp.zeros((half, width), F32)
        for w in range(terms):
            if gather_right:
                b = rbuf[:, w * ncol:(w + 1) * ncol, :].reshape(width, width)
                total = total + lax.dot_general(inner[w, at], b, NT, preferred_element_type=F32)
            else:
                total = total + lax.dot_general(
                    inner[w, at], right_ref[w], NN, preferred_element_type=F32
                )
        return total * mask[at]

    reduce_start(0)
    halo1 = halo(live, 0)
    next(halo1)
    next(halo1)
    gathers = [gather(lbuf, nr, ri, lambda r: (li, r), l_send, l_recv, False)]
    if gather_right:
        gathers.append(gather(rbuf, nl, li, lambda l: (l, ri), r_send, r_recv, True))
    for g in gathers:
        next(g)
    reduce_middle(0)
    next(halo1)
    steps = [nr // 2 - 1, nl // 2 - 1][:len(gathers)]
    for s in range(max(steps)):
        for g, n in zip(gathers, steps):
            if s < n:
                next(g)
        if s == 0:
            next(halo1)
    for _ in halo1:
        pass
    scale = lax.rsqrt(reduce_end(0)[0:1] / count + 1e-06)
    for k in range(9):
        first[k] = (live[k].astype(F32) * scale).astype(BF16)
    for _ in gathers[0]:
        pass
    apply_left(first)
    for g in gathers[1:]:
        for _ in g:
            pass
    half = width // 2
    halo2 = halo(images, 1)
    for c in range(2):
        at = slice(c * half, (c + 1) * half)
        w1 = apply_right(c)
        w1_ref[at] = w1
        w1_bf16 = w1.astype(BF16)
        images[4, at] = w1_bf16
        next(halo2)
        image1_ref[at] = w1_bf16
    w1 = w1_ref[...]
    v1 = first[4].astype(F32)
    part[1, 0:1, :] = lanes(v1 * w1)
    part[1, 1:2, :] = lanes(w1 * w1)
    part[1, 2:3, :] = lanes(v1 * v1)
    reduce_start(1)
    next(halo2)
    reduce_middle(1)
    for _ in halo2:
        pass
    apply_left(images)
    sums = reduce_end(1)
    alpha = sums[0:1] / count
    nr_ = sums[1:2] / count - 2.0 * alpha * alpha + alpha * alpha * (sums[2:3] / count)
    factor = lax.rsqrt(jnp.maximum(nr_, 0.0) + 1e-06)
    totals = [jnp.zeros((1, 128), F32)] * 3
    for c in range(2):
        at = slice(c * half, (c + 1) * half)
        w1 = w1_ref[at]
        w2 = (apply_right(c) - alpha * w1) * factor
        image2_ref[at] = w2.astype(BF16)
        v1 = first[4, at].astype(F32)
        v2 = ((w1 - alpha * v1) * factor).astype(BF16).astype(F32)
        products = (v1 * w2, v2 * w1, v2 * w2)
        totals = [total + lanes(product) for total, product in zip(totals, products)]
    for k in range(3):
        part[2, k:k + 1, :] = totals[k]
    reduce_start(2)
    reduce_middle(2)
    sums = reduce_end(2) / count
    r8 = lax.broadcasted_iota(jnp.int32, (8, 128), 0)
    c8 = lax.broadcasted_iota(jnp.int32, (8, 128), 1)
    top = jnp.where(c8 == 0, alpha, sums[0:1])
    bottom = jnp.where(c8 == 0, sums[1:2], sums[2:3])
    proj_ref[...] = jnp.where(r8 == 0, top, bottom)[:2, :2]

    for copy, cond in pending:
        when(cond, copy.wait_send)


def on_device(nl, nr, psi, left_env, right_env, left_dims, right_dims, term_shift):
    width = psi.shape[0]
    terms = left_env.shape[0]
    mine = left_env.shape[1]
    ncol = right_env.shape[2]
    gather_right = ncol % 16 == 0
    left = left_env.reshape(terms * mine, width)
    if gather_right:
        right = jnp.swapaxes(right_env, 1, 2).reshape(terms * ncol, width)
        rshape = (nl, terms * ncol, width)
    else:
        right = lax.all_gather(right_env, "lsec", axis=2, tiled=True)
        rshape = (1, 16, 128)
    vmem = pl.BlockSpec(memory_space=pltpu.VMEM)
    smem = pl.BlockSpec(memory_space=pltpu.SMEM)
    dma = pltpu.SemaphoreType.DMA
    image1, image2, proj = pl.pallas_call(
        functools.partial(kernel, nl, nr, gather_right, terms),
        out_shape=(
            jax.ShapeDtypeStruct((width, width), BF16),
            jax.ShapeDtypeStruct((width, width), BF16),
            jax.ShapeDtypeStruct((2, 2), F32),
        ),
        in_specs=[smem] * 3 + [vmem] * 3,
        out_specs=(vmem, vmem, vmem),
        scratch_shapes=[
            pltpu.VMEM((9, width, width), BF16),
            pltpu.VMEM((9, width, width), BF16),
            pltpu.VMEM((9, width, width), BF16),
            pltpu.VMEM((terms, width, width), BF16),
            pltpu.VMEM((nr, terms * mine, width), BF16),
            pltpu.VMEM(rshape, BF16),
            pltpu.VMEM((width, width), F32),
            pltpu.VMEM((3, 8, 128), F32),
            pltpu.VMEM((3, 8, 128), F32),
            pltpu.VMEM((3, nr, 8, 128), F32),
            pltpu.VMEM((3, nl, 8, 128), F32),
            dma((3, 2, nr)),
            dma((2, nr)),
            dma((4, 2, nl)),
            dma((2, nl)),
            dma((2, 2, 9)),
            dma((2, 2, 9)),
            dma((3, nr)),
            dma((3, nr)),
            dma((3, nl)),
            dma((3, nl)),
        ],
        compiler_params=pltpu.CompilerParams(
            collective_id=0, has_side_effects=True, vmem_limit_bytes=40 * 1024 * 1024
        ),
        cost_estimate=pl.CostEstimate(
            flops=8 * terms * width**3, bytes_accessed=4 * 2**20, transcendentals=2
        ),
    )(term_shift.T, left_dims, right_dims, psi, left, right)
    return image1, image2, proj


def solution(mesh):
    nl, nr = mesh.shape["lsec"], mesh.shape["rsec"]
    in_specs = (
        P("lsec", "rsec"),
        P(None, ("lsec", "rsec"), None),
        P(None, "rsec", "lsec"),
        P("lsec"),
        P("rsec"),
        P(),
    )
    out_specs = (P("lsec", "rsec"), P("lsec", "rsec"), P())
    return jax.shard_map(
        functools.partial(on_device, nl, nr),
        mesh=mesh, in_specs=in_specs, out_specs=out_specs, check_vma=False,
    )
```

```python
import functools

import jax
import jax.numpy as jnp
from jax import lax
from jax.experimental import pallas as pl
from jax.experimental.pallas import tpu as pltpu
from jax.sharding import PartitionSpec as P

MESH = pl.DeviceIdType.MESH
F32 = jnp.float32
BF16 = jnp.bfloat16
NT = (((1,), (1,)), ((), ()))
NN = (((1,), (0,)), ((), ()))


def kernel(
    nl, nr, gather_right, terms,
    shift_ref, ldim_ref, rdim_ref, psi_hbm, left_hbm, right_hbm,
    image1_ref, image2_ref, proj_ref,
    psi_ref, live, first, images, inner, lbuf, rbuf, w1_ref, part, row_sum, row_slots, col_slots,
    l_send, l_recv, r_send, r_recv, h_send, h_recv, ar_send, ar_recv, ac_send, ac_recv, own_sem,
):
    width = psi_hbm.shape[0]
    count = float(nl * nr * width * width)
    li, ri = lax.axis_index("lsec"), lax.axis_index("rsec")
    pending = []
    own = [
        pltpu.make_async_copy(psi_hbm, psi_ref, own_sem.at[0]),
        pltpu.make_async_copy(left_hbm, lbuf.at[ri], own_sem.at[1]),
        pltpu.make_async_copy(right_hbm, rbuf.at[li] if gather_right else rbuf, own_sem.at[2]),
    ]
    for copy in own:
        copy.start()

    def when(cond, fn):
        if cond is None:
            fn()
        else:
            pl.when(cond)(fn)

    def send(src, dst, send_sem, recv_sem, device, cond=None):
        copy = pltpu.make_async_remote_copy(
            src_ref=src, dst_ref=dst, send_sem=send_sem, recv_sem=recv_sem,
            device_id=device, device_id_type=MESH,
        )
        when(cond, copy.start)
        pending.append((copy, cond))

    def arrive(dst, send_sem, recv_sem, device, cond=None):
        copy = pltpu.make_async_remote_copy(
            src_ref=dst, dst_ref=dst, send_sem=send_sem, recv_sem=recv_sem,
            device_id=device, device_id_type=MESH,
        )
        when(cond, copy.wait_recv)

    def drain(n):
        for copy, cond in pending[:n]:
            when(cond, copy.wait_send)
        del pending[:n]

    barrier = pltpu.get_barrier_semaphore()

    def greet_col(i, _):
        pl.semaphore_signal(
            barrier, inc=1, device_id=(lax.rem(li + i, nl), ri), device_id_type=MESH
        )
        return 0

    def greet_row(i, _):
        pl.semaphore_signal(
            barrier, inc=1, device_id=(li, lax.rem(ri + i, nr)), device_id_type=MESH
        )
        return 0

    lax.fori_loop(1, nl, greet_col, 0)
    lax.fori_loop(1, nr, greet_row, 0)

    rows = lax.broadcasted_iota(jnp.int32, (width, width), 0)
    cols = lax.broadcasted_iota(jnp.int32, (width, width), 1)
    mask = ((rows < ldim_ref[0]) & (cols < rdim_ref[0])).astype(F32)

    def lanes(x):
        total = jnp.sum(x, axis=0, keepdims=True)
        out = total[:, 0:128]
        for at in range(128, width, 128):
            out = out + total[:, at:at + 128]
        return out

    own[0].wait()
    live32 = psi_ref[...].astype(F32) * mask
    live[4] = live32.astype(BF16)
    part[...] = jnp.zeros_like(part)
    part[0, 0:1, :] = lanes(live32 * live32)


    for store in (live, images):
        for k in range(9):
            dl, dr = k // 3 - 1, k % 3 - 1
            outside = (li - dl < 0) | (li - dl >= nl) | (ri - dr < 0) | (ri - dr >= nr)
            if k != 4:
                def clear(store=store, k=k):
                    store[k] = jnp.zeros((width, width), BF16)
                pl.when(outside)(clear)

    pl.semaphore_wait(barrier, nl + nr - 2)

    def reduce_start(t):
        for i in range(1, nr):
            other = lax.rem(ri + i, nr)
            send(part.at[t], row_slots.at[t, ri], ar_send.at[t, i], ar_recv.at[t, ri], (li, other))

    def reduce_middle(t):
        for i in range(1, nr):
            other = lax.rem(ri + i, nr)
            arrive(row_slots.at[t, other], ar_send.at[t, i], ar_recv.at[t, other], (li, other))
        row_slots[t, pl.ds(ri, 1)] = part[t][None]
        total = row_slots[t, 0]
        for i in range(1, nr):
            total = total + row_slots[t, i]
        row_sum[t] = total
        for i in range(1, nl):
            other = lax.rem(li + i, nl)
            send(row_sum.at[t], col_slots.at[t, li], ac_send.at[t, i], ac_recv.at[t, li], (other, ri))

    def reduce_end(t):
        for i in range(1, nl):
            other = lax.rem(li + i, nl)
            arrive(col_slots.at[t, other], ac_send.at[t, i], ac_recv.at[t, other], (other, ri))
        col_slots[t, pl.ds(li, 1)] = row_sum[t][None]
        total = col_slots[t, 0]
        for i in range(1, nl):
            total = total + col_slots[t, i]
        return jnp.sum(total, axis=1, keepdims=True)

    def gather(mine, buf, n, me, device, send_sem, recv_sem, parts, balance):
        outer = n // 2
        o, i = me // 2, lax.rem(me, 2)
        pair = me + 1 - 2 * i
        pair_dev = device(pair)
        balance = balance and parts == 2 and outer > 2 and outer % 2 == 0
        mate = o + 1 - 2 * lax.rem(o, 2)
        size = buf.shape[1] // parts

        def piece(at, h):
            return buf.at[at, pl.ds(h * size, size)]

        def put(at, h, sem, dev, cond, src=None):
            src = piece(at, h) if src is None else src
            send(src, piece(at, h), sem, recv_sem.at[h, at], dev, cond)

        def got(at, h, cond=None):
            arrive(piece(at, h), send_sem.at[2, h, 0], recv_sem.at[h, at], pair_dev, cond)

        def forward(slot, h, cond=None):
            if balance and h == 1:
                cond = (slot != mate) if cond is None else cond & (slot != mate)
            put(slot * 2 + i, h, send_sem.at[2, h, slot], pair_dev, cond)

        for h in range(parts):
            put(me, h, send_sem.at[2, h, o], pair_dev, None, mine.at[pl.ds(h * size, size)])
        for s in range(outer - 1):
            low, high = o - s, o + s
            up = device(jnp.minimum(me + 2, n - 1))
            down = device(jnp.maximum(me - 2, 0))
            for h in range(parts):
                src = mine.at[pl.ds(h * size, size)] if s == 0 else None
                put(jnp.maximum(low, 0) * 2 + i, h, send_sem.at[0, h, s], up,
                    (low >= 0) & (o < outer - 1), src)
                put(jnp.minimum(high, outer - 1) * 2 + i, h, send_sem.at[1, h, s], down,
                    (high < outer) & (o > 0), src)
            if balance and s == 1:
                got(o * 2 + 1 - i, 1)
                put(o * 2 + 1 - i, 1, send_sem.at[3, 0, 0], device(mate * 2 + i), None)
            yield
            for h in range(parts):
                for slot, cond in ((low - 1, low - 1 >= 0), (high + 1, high + 1 < outer)):
                    slot = jnp.clip(slot, 0, outer - 1)
                    got(slot * 2 + i, h, cond)
                    forward(slot, h, cond)
        yield
        for slot in range(outer):
            for h in range(parts):
                early = balance and h == 1
                got(slot * 2 + 1 - i, h, (slot != o) if early else None)

    def halo(buf, t, chunks):
        outer = nl // 2
        o, i = li // 2, lax.rem(li, 2)
        from_pair, from_line = 1 + 6 * i, 7 - 6 * i
        pair = (li + 1 - 2 * i, ri)
        onward = (jnp.clip(li + 2 - 4 * i, 0, nl - 1), ri)
        goes = ((i == 0) & (o < outer - 1)) | ((i == 1) & (o > 0))
        comes = ((i == 0) & (o > 0)) | ((i == 1) & (o < outer - 1))
        east, west = (li, jnp.minimum(ri + 1, nr - 1)), (li, jnp.maximum(ri - 1, 0))
        size = width // chunks

        def piece(k, c):
            return buf.at[k, pl.ds(c * size, size)]

        def put(src, dst, c, sem, dev, cond=None):
            send(piece(src, c), piece(dst, c), h_send.at[t, c, sem], h_recv.at[t, c, dst], dev, cond)

        def got(k, c, cond=None):
            arrive(piece(k, c), h_send.at[t, c, k], h_recv.at[t, c, k], pair, cond)

        def sideways(k, c, cond):
            go = ri < nr - 1
            put(k, k + 1, c, k + 1, east, go if cond is None else go & cond)
            go = ri > 0
            put(k, k - 1, c, k - 1, west, go if cond is None else go & cond)

        for c in range(chunks):
            put(4, from_line, c, 4, pair)
            sideways(4, c, None)
            yield
        for c in range(chunks):
            got(from_pair, c)
            put(from_pair, from_line, c, from_pair, onward, goes)
            sideways(from_pair, c, None)
        yield
        for c in range(chunks):
            got(from_line, c, comes)
            sideways(from_line, c, comes)
        yield
        for c in range(chunks):
            for k, l_ok in ((4, None), (from_pair, None), (from_line, comes)):
                for at, r_ok in ((k + 1, ri > 0), (k - 1, ri < nr - 1)):
                    got(at, c, r_ok if l_ok is None else r_ok & l_ok)

    def apply_left(vec):
        def term(w, _):
            k = (shift_ref[0, w] + 1) * 3 + shift_ref[1, w] + 1
            product = jnp.dot(
                lbuf[:, w].reshape(width, width), vec[k], preferred_element_type=F32
            )
            inner[w] = product.astype(BF16)
            return 0

        lax.fori_loop(0, terms, term, 0, unroll=2)

    def apply_right(c):
        half = width // 2
        at = slice(c * half, (c + 1) * half)

        def term(w, total):
            if gather_right:
                b, dims = rbuf[:, w].reshape(width, width), NT
            else:
                b, dims = rbuf[w], NN
            return total + lax.dot_general(inner[w, at], b, dims, preferred_element_type=F32)

        total = lax.fori_loop(0, terms, term, jnp.zeros((half, width), F32), unroll=2)
        return total * mask[at]

    reduce_start(0)
    halo1 = halo(live, 0, 1)
    next(halo1)
    gathers = [gather(left_hbm, lbuf, nr, ri, lambda r: (li, r), l_send, l_recv, 1, False)]
    if gather_right:
        gathers.append(
            gather(right_hbm, rbuf, nl, li, lambda l: (l, ri), r_send, r_recv, 2, True)
        )
    for g in gathers:
        next(g)
    reduce_middle(0)
    next(halo1)
    steps = [nr // 2 - 1, nl // 2 - 1][:len(gathers)]
    for s in range(max(steps)):
        for g, n in zip(gathers, steps):
            if s < n:
                next(g)
        if s == 0:
            next(halo1)
    for _ in halo1:
        pass
    scale = lax.rsqrt(reduce_end(0)[0:1] / count + 1e-06)
    for k in range(9):
        first[k] = (live[k].astype(F32) * scale).astype(BF16)
    for _ in gathers[0]:
        pass
    own[1].wait()
    apply_left(first)
    own[2].wait()
    for g in gathers[1:]:
        for _ in g:
            pass
    half = width // 2
    early = len(pending)
    halo2 = halo(images, 1, 2)
    for c in range(2):
        at = slice(c * half, (c + 1) * half)
        w1 = apply_right(c)
        w1_ref[at] = w1
        w1_bf16 = w1.astype(BF16)
        images[4, at] = w1_bf16
        next(halo2)
        image1_ref[at] = w1_bf16
    w1 = w1_ref[...]
    v1 = first[4].astype(F32)
    part[1, 0:1, :] = lanes(v1 * w1)
    part[1, 1:2, :] = lanes(w1 * w1)
    part[1, 2:3, :] = lanes(v1 * v1)
    reduce_start(1)
    next(halo2)
    reduce_middle(1)
    next(halo2)
    drain(early)
    for _ in halo2:
        pass
    apply_left(images)
    sums = reduce_end(1)
    alpha = sums[0:1] / count
    nr_ = sums[1:2] / count - 2.0 * alpha * alpha + alpha * alpha * (sums[2:3] / count)
    factor = lax.rsqrt(jnp.maximum(nr_, 0.0) + 1e-06)
    totals = [jnp.zeros((1, 128), F32)] * 3
    for c in range(2):
        at = slice(c * half, (c + 1) * half)
        w1 = w1_ref[at]
        w2 = (apply_right(c) - alpha * w1) * factor
        image2_ref[at] = w2.astype(BF16)
        v1 = first[4, at].astype(F32)
        v2 = ((w1 - alpha * v1) * factor).astype(BF16).astype(F32)
        products = (v1 * w2, v2 * w1, v2 * w2)
        totals = [total + lanes(product) for total, product in zip(totals, products)]
    for k in range(3):
        part[2, k:k + 1, :] = totals[k]
    reduce_start(2)
    reduce_middle(2)
    sums = reduce_end(2) / count
    r8 = lax.broadcasted_iota(jnp.int32, (8, 128), 0)
    c8 = lax.broadcasted_iota(jnp.int32, (8, 128), 1)
    top = jnp.where(c8 == 0, alpha, sums[0:1])
    bottom = jnp.where(c8 == 0, sums[1:2], sums[2:3])
    proj_ref[...] = jnp.where(r8 == 0, top, bottom)[:2, :2]

    drain(len(pending))


def on_device(nl, nr, psi, left_env, right_env, left_dims, right_dims, term_shift):
    width = psi.shape[0]
    terms = left_env.shape[0]
    mine = left_env.shape[1]
    ncol = right_env.shape[2]
    gather_right = ncol % 16 == 0
    if gather_right:
        right = jnp.swapaxes(right_env, 1, 2)
        rshape = (nl, terms, ncol, width)
    else:
        right = lax.all_gather(right_env, "lsec", axis=2, tiled=True)
        rshape = (terms, width, width)
    vmem = pl.BlockSpec(memory_space=pltpu.VMEM)
    hbm = pl.BlockSpec(memory_space=pl.ANY)
    smem = pl.BlockSpec(memory_space=pltpu.SMEM)
    dma = pltpu.SemaphoreType.DMA
    image1, image2, proj = pl.pallas_call(
        functools.partial(kernel, nl, nr, gather_right, terms),
        out_shape=(
            jax.ShapeDtypeStruct((width, width), BF16),
            jax.ShapeDtypeStruct((width, width), BF16),
            jax.ShapeDtypeStruct((2, 2), F32),
        ),
        in_specs=[smem] * 3 + [hbm] * 3,
        out_specs=(vmem, vmem, vmem),
        scratch_shapes=[
            pltpu.VMEM((width, width), BF16),
            pltpu.VMEM((9, width, width), BF16),
            pltpu.VMEM((9, width, width), BF16),
            pltpu.VMEM((9, width, width), BF16),
            pltpu.VMEM((terms, width, width), BF16),
            pltpu.VMEM((nr, terms, mine, width), BF16),
            pltpu.VMEM(rshape, BF16),
            pltpu.VMEM((width, width), F32),
            pltpu.VMEM((3, 8, 128), F32),
            pltpu.VMEM((3, 8, 128), F32),
            pltpu.VMEM((3, nr, 8, 128), F32),
            pltpu.VMEM((3, nl, 8, 128), F32),
            dma((3, 2, nr)),
            dma((2, nr)),
            dma((4, 2, nl)),
            dma((2, nl)),
            dma((2, 2, 9)),
            dma((2, 2, 9)),
            dma((3, nr)),
            dma((3, nr)),
            dma((3, nl)),
            dma((3, nl)),
            dma((3,)),
        ],
        compiler_params=pltpu.CompilerParams(
            collective_id=0, has_side_effects=True, vmem_limit_bytes=56 * 1024 * 1024
        ),
        cost_estimate=pl.CostEstimate(
            flops=8 * terms * width**3, bytes_accessed=4 * 2**20, transcendentals=2
        ),
    )(term_shift.T, left_dims, right_dims, psi, left_env, right)
    return image1, image2, proj


def solution(mesh):
    nl, nr = mesh.shape["lsec"], mesh.shape["rsec"]
    in_specs = (
        P("lsec", "rsec"),
        P(None, ("lsec", "rsec"), None),
        P(None, "rsec", "lsec"),
        P("lsec"),
        P("rsec"),
        P(),
    )
    out_specs = (P("lsec", "rsec"), P("lsec", "rsec"), P())
    return jax.shard_map(
        functools.partial(on_device, nl, nr),
        mesh=mesh, in_specs=in_specs, out_specs=out_specs, check_vma=False,
    )
```

```python
import functools

import jax
import jax.numpy as jnp
from jax import lax
from jax.experimental import pallas as pl
from jax.experimental.pallas import tpu as pltpu
from jax.sharding import PartitionSpec as P

MESH = pl.DeviceIdType.MESH
F32 = jnp.float32
BF16 = jnp.bfloat16
NT = (((1,), (1,)), ((), ()))
NN = (((1,), (0,)), ((), ()))


def kernel(
    nl, nr, gather_right, terms,
    shift_ref, ldim_ref, rdim_ref, psi_hbm, left_hbm, right_hbm,
    image1_ref, image2_ref, proj_ref,
    psi_ref, live, first, images, inner, lbuf, rbuf, w1_ref, part, row_sum, row_slots, col_slots,
    l_send, l_recv, r_send, r_recv, h_send, h_recv, ar_send, ar_recv, ac_send, ac_recv, own_sem,
):
    width = psi_hbm.shape[0]
    count = float(nl * nr * width * width)
    li, ri = lax.axis_index("lsec"), lax.axis_index("rsec")
    pending = []
    own = [
        pltpu.make_async_copy(psi_hbm, psi_ref, own_sem.at[0]),
        pltpu.make_async_copy(left_hbm, lbuf.at[ri], own_sem.at[1]),
        pltpu.make_async_copy(right_hbm, rbuf.at[li] if gather_right else rbuf, own_sem.at[2]),
    ]
    for copy in own:
        copy.start()

    def when(cond, fn):
        if cond is None:
            fn()
        else:
            pl.when(cond)(fn)

    def send(src, dst, send_sem, recv_sem, device, cond=None):
        copy = pltpu.make_async_remote_copy(
            src_ref=src, dst_ref=dst, send_sem=send_sem, recv_sem=recv_sem,
            device_id=device, device_id_type=MESH,
        )
        when(cond, copy.start)
        pending.append((copy, cond))

    def arrive(dst, send_sem, recv_sem, device, cond=None):
        copy = pltpu.make_async_remote_copy(
            src_ref=dst, dst_ref=dst, send_sem=send_sem, recv_sem=recv_sem,
            device_id=device, device_id_type=MESH,
        )
        when(cond, copy.wait_recv)

    def drain(n):
        for copy, cond in pending[:n]:
            when(cond, copy.wait_send)
        del pending[:n]

    barrier = pltpu.get_barrier_semaphore()

    def greet_col(i, _):
        pl.semaphore_signal(
            barrier, inc=1, device_id=(lax.rem(li + i, nl), ri), device_id_type=MESH
        )
        return 0

    def greet_row(i, _):
        pl.semaphore_signal(
            barrier, inc=1, device_id=(li, lax.rem(ri + i, nr)), device_id_type=MESH
        )
        return 0

    lax.fori_loop(1, nl, greet_col, 0)
    lax.fori_loop(1, nr, greet_row, 0)

    rows = lax.broadcasted_iota(jnp.int32, (width, width), 0)
    cols = lax.broadcasted_iota(jnp.int32, (width, width), 1)
    mask = ((rows < ldim_ref[0]) & (cols < rdim_ref[0])).astype(F32)

    def lanes(x):
        total = jnp.sum(x, axis=0, keepdims=True)
        out = total[:, 0:128]
        for at in range(128, width, 128):
            out = out + total[:, at:at + 128]
        return out

    own[0].wait()
    live32 = psi_ref[...].astype(F32) * mask
    live[4] = live32.astype(BF16)
    part[...] = jnp.zeros_like(part)
    part[0, 0:1, :] = lanes(live32 * live32)


    for store in (live, images):
        for k in range(9):
            dl, dr = k // 3 - 1, k % 3 - 1
            outside = (li - dl < 0) | (li - dl >= nl) | (ri - dr < 0) | (ri - dr >= nr)
            if k != 4:
                def clear(store=store, k=k):
                    store[k] = jnp.zeros((width, width), BF16)
                pl.when(outside)(clear)

    pl.semaphore_wait(barrier, nl + nr - 2)

    def reduce_start(t):
        for i in range(1, nr):
            other = lax.rem(ri + i, nr)
            send(part.at[t], row_slots.at[t, ri], ar_send.at[t, i], ar_recv.at[t, ri], (li, other))

    def reduce_middle(t):
        for i in range(1, nr):
            other = lax.rem(ri + i, nr)
            arrive(row_slots.at[t, other], ar_send.at[t, i], ar_recv.at[t, other], (li, other))
        row_slots[t, pl.ds(ri, 1)] = part[t][None]
        total = row_slots[t, 0]
        for i in range(1, nr):
            total = total + row_slots[t, i]
        row_sum[t] = total
        for i in range(1, nl):
            other = lax.rem(li + i, nl)
            send(row_sum.at[t], col_slots.at[t, li], ac_send.at[t, i], ac_recv.at[t, li], (other, ri))

    def reduce_end(t):
        for i in range(1, nl):
            other = lax.rem(li + i, nl)
            arrive(col_slots.at[t, other], ac_send.at[t, i], ac_recv.at[t, other], (other, ri))
        col_slots[t, pl.ds(li, 1)] = row_sum[t][None]
        total = col_slots[t, 0]
        for i in range(1, nl):
            total = total + col_slots[t, i]
        return jnp.sum(total, axis=1, keepdims=True)

    def gather(mine, buf, n, me, device, send_sem, recv_sem, parts, balance):
        outer = n // 2
        o, i = me // 2, lax.rem(me, 2)
        pair = me + 1 - 2 * i
        pair_dev = device(pair)
        balance = balance and parts == 2 and outer > 2 and outer % 2 == 0
        mate = o + 1 - 2 * lax.rem(o, 2)
        size = buf.shape[1] // parts

        def piece(at, h):
            return buf.at[at, pl.ds(h * size, size)]

        def put(at, h, sem, dev, cond, src=None):
            src = piece(at, h) if src is None else src
            send(src, piece(at, h), sem, recv_sem.at[h, at], dev, cond)

        def got(at, h, cond=None):
            arrive(piece(at, h), send_sem.at[2, h, 0], recv_sem.at[h, at], pair_dev, cond)

        def forward(slot, h, cond=None):
            if balance and h == 1:
                cond = (slot != mate) if cond is None else cond & (slot != mate)
            put(slot * 2 + i, h, send_sem.at[2, h, slot], pair_dev, cond)

        for s in range(outer - 1):
            low, high = o - s, o + s
            up = device(jnp.minimum(me + 2, n - 1))
            down = device(jnp.maximum(me - 2, 0))
            for h in range(parts):
                src = mine.at[pl.ds(h * size, size)] if s == 0 else None
                put(jnp.maximum(low, 0) * 2 + i, h, send_sem.at[0, h, s], up,
                    (low >= 0) & (o < outer - 1), src)
                put(jnp.minimum(high, outer - 1) * 2 + i, h, send_sem.at[1, h, s], down,
                    (high < outer) & (o > 0), src)
            if s == 0:
                for h in range(parts):
                    put(me, h, send_sem.at[2, h, o], pair_dev, None, mine.at[pl.ds(h * size, size)])
            if balance and s == 1:
                got(o * 2 + 1 - i, 1)
                put(o * 2 + 1 - i, 1, send_sem.at[3, 0, 0], device(mate * 2 + i), None)
            yield
            for h in range(parts):
                for slot, cond in ((low - 1, low - 1 >= 0), (high + 1, high + 1 < outer)):
                    slot = jnp.clip(slot, 0, outer - 1)
                    got(slot * 2 + i, h, cond)
                    forward(slot, h, cond)
        yield
        for slot in range(outer):
            for h in range(parts):
                early = balance and h == 1
                got(slot * 2 + 1 - i, h, (slot != o) if early else None)

    def halo(buf, t, chunks):
        outer = nl // 2
        o, i = li // 2, lax.rem(li, 2)
        from_pair, from_line = 1 + 6 * i, 7 - 6 * i
        pair = (li + 1 - 2 * i, ri)
        onward = (jnp.clip(li + 2 - 4 * i, 0, nl - 1), ri)
        goes = ((i == 0) & (o < outer - 1)) | ((i == 1) & (o > 0))
        comes = ((i == 0) & (o > 0)) | ((i == 1) & (o < outer - 1))
        east, west = (li, jnp.minimum(ri + 1, nr - 1)), (li, jnp.maximum(ri - 1, 0))
        size = width // chunks

        def piece(k, c):
            return buf.at[k, pl.ds(c * size, size)]

        def put(src, dst, c, sem, dev, cond=None):
            send(piece(src, c), piece(dst, c), h_send.at[t, c, sem], h_recv.at[t, c, dst], dev, cond)

        def got(k, c, cond=None):
            arrive(piece(k, c), h_send.at[t, c, k], h_recv.at[t, c, k], pair, cond)

        def sideways(k, c, cond):
            go = ri < nr - 1
            put(k, k + 1, c, k + 1, east, go if cond is None else go & cond)
            go = ri > 0
            put(k, k - 1, c, k - 1, west, go if cond is None else go & cond)

        for c in range(chunks):
            put(4, from_line, c, 4, pair)
            sideways(4, c, None)
            yield
        for c in range(chunks):
            got(from_pair, c)
            put(from_pair, from_line, c, from_pair, onward, goes)
            sideways(from_pair, c, None)
        yield
        for c in range(chunks):
            got(from_line, c, comes)
            sideways(from_line, c, comes)
        yield
        for c in range(chunks):
            for k, l_ok in ((4, None), (from_pair, None), (from_line, comes)):
                for at, r_ok in ((k + 1, ri > 0), (k - 1, ri < nr - 1)):
                    got(at, c, r_ok if l_ok is None else r_ok & l_ok)

    def apply_left(vec):
        def term(w, _):
            k = (shift_ref[0, w] + 1) * 3 + shift_ref[1, w] + 1
            product = jnp.dot(
                lbuf[:, w].reshape(width, width), vec[k], preferred_element_type=F32
            )
            inner[w] = product.astype(BF16)
            return 0

        lax.fori_loop(0, terms, term, 0, unroll=2)

    def apply_right(c):
        half = width // 2
        at = slice(c * half, (c + 1) * half)

        def term(w, total):
            if gather_right:
                b, dims = rbuf[:, w].reshape(width, width), NT
            else:
                b, dims = rbuf[w], NN
            return total + lax.dot_general(inner[w, at], b, dims, preferred_element_type=F32)

        total = lax.fori_loop(0, terms, term, jnp.zeros((half, width), F32), unroll=2)
        return total * mask[at]

    reduce_start(0)
    left = gather(left_hbm, lbuf, nr, ri, lambda r: (li, r), l_send, l_recv, 1, False)
    right = iter(())
    if gather_right:
        right = gather(right_hbm, rbuf, nl, li, lambda l: (l, ri), r_send, r_recv, 2, True)
    halo1 = halo(live, 0, 1)
    next(right, None)
    next(halo1)
    next(left)
    next(right, None)
    next(halo1)
    reduce_middle(0)
    next(left, None)
    next(right, None)
    next(halo1)
    for _ in range(nl // 2 - 3):
        next(right, None)
    for _ in halo1:
        pass
    scale = lax.rsqrt(reduce_end(0)[0:1] / count + 1e-06)
    for k in range(9):
        first[k] = (live[k].astype(F32) * scale).astype(BF16)
    for _ in left:
        pass
    own[1].wait()
    apply_left(first)
    own[2].wait()
    for _ in right:
        pass
    half = width // 2
    early = len(pending)
    halo2 = halo(images, 1, 2)
    for c in range(2):
        at = slice(c * half, (c + 1) * half)
        w1 = apply_right(c)
        w1_ref[at] = w1
        w1_bf16 = w1.astype(BF16)
        images[4, at] = w1_bf16
        next(halo2)
        image1_ref[at] = w1_bf16
    w1 = w1_ref[...]
    v1 = first[4].astype(F32)
    part[1, 0:1, :] = lanes(v1 * w1)
    part[1, 1:2, :] = lanes(w1 * w1)
    part[1, 2:3, :] = lanes(v1 * v1)
    reduce_start(1)
    next(halo2)
    reduce_middle(1)
    next(halo2)
    drain(early)
    for _ in halo2:
        pass
    apply_left(images)
    sums = reduce_end(1)
    alpha = sums[0:1] / count
    nr_ = sums[1:2] / count - 2.0 * alpha * alpha + alpha * alpha * (sums[2:3] / count)
    factor = lax.rsqrt(jnp.maximum(nr_, 0.0) + 1e-06)
    totals = [jnp.zeros((1, 128), F32)] * 3
    for c in range(2):
        at = slice(c * half, (c + 1) * half)
        w1 = w1_ref[at]
        w2 = (apply_right(c) - alpha * w1) * factor
        image2_ref[at] = w2.astype(BF16)
        v1 = first[4, at].astype(F32)
        v2 = ((w1 - alpha * v1) * factor).astype(BF16).astype(F32)
        products = (v1 * w2, v2 * w1, v2 * w2)
        totals = [total + lanes(product) for total, product in zip(totals, products)]
    for k in range(3):
        part[2, k:k + 1, :] = totals[k]
    reduce_start(2)
    reduce_middle(2)
    sums = reduce_end(2) / count
    r8 = lax.broadcasted_iota(jnp.int32, (8, 128), 0)
    c8 = lax.broadcasted_iota(jnp.int32, (8, 128), 1)
    top = jnp.where(c8 == 0, alpha, sums[0:1])
    bottom = jnp.where(c8 == 0, sums[1:2], sums[2:3])
    proj_ref[...] = jnp.where(r8 == 0, top, bottom)[:2, :2]

    drain(len(pending))


def on_device(nl, nr, psi, left_env, right_env, left_dims, right_dims, term_shift):
    width = psi.shape[0]
    terms = left_env.shape[0]
    mine = left_env.shape[1]
    ncol = right_env.shape[2]
    gather_right = ncol % 16 == 0
    if gather_right:
        right = jnp.swapaxes(right_env, 1, 2)
        rshape = (nl, terms, ncol, width)
    else:
        right = lax.all_gather(right_env, "lsec", axis=2, tiled=True)
        rshape = (terms, width, width)
    vmem = pl.BlockSpec(memory_space=pltpu.VMEM)
    hbm = pl.BlockSpec(memory_space=pltpu.HBM)
    smem = pl.BlockSpec(memory_space=pltpu.SMEM)
    dma = pltpu.SemaphoreType.DMA
    image1, image2, proj = pl.pallas_call(
        functools.partial(kernel, nl, nr, gather_right, terms),
        out_shape=(
            jax.ShapeDtypeStruct((width, width), BF16),
            jax.ShapeDtypeStruct((width, width), BF16),
            jax.ShapeDtypeStruct((2, 2), F32),
        ),
        in_specs=[smem] * 3 + [hbm] * 3,
        out_specs=(vmem, vmem, vmem),
        scratch_shapes=[
            pltpu.VMEM((width, width), BF16),
            pltpu.VMEM((9, width, width), BF16),
            pltpu.VMEM((9, width, width), BF16),
            pltpu.VMEM((9, width, width), BF16),
            pltpu.VMEM((terms, width, width), BF16),
            pltpu.VMEM((nr, terms, mine, width), BF16),
            pltpu.VMEM(rshape, BF16),
            pltpu.VMEM((width, width), F32),
            pltpu.VMEM((3, 8, 128), F32),
            pltpu.VMEM((3, 8, 128), F32),
            pltpu.VMEM((3, nr, 8, 128), F32),
            pltpu.VMEM((3, nl, 8, 128), F32),
            dma((3, 2, nr)),
            dma((2, nr)),
            dma((4, 2, nl)),
            dma((2, nl)),
            dma((2, 2, 9)),
            dma((2, 2, 9)),
            dma((3, nr)),
            dma((3, nr)),
            dma((3, nl)),
            dma((3, nl)),
            dma((3,)),
        ],
        compiler_params=pltpu.CompilerParams(
            collective_id=0, has_side_effects=True, vmem_limit_bytes=32 * 1024 * 1024
        ),
        cost_estimate=pl.CostEstimate(
            flops=8 * terms * width**3, bytes_accessed=4 * 2**20, transcendentals=2
        ),
    )(term_shift.T, left_dims, right_dims, psi, left_env, right)
    return image1, image2, proj


def solution(mesh):
    nl, nr = mesh.shape["lsec"], mesh.shape["rsec"]
    in_specs = (
        P("lsec", "rsec"),
        P(None, ("lsec", "rsec"), None),
        P(None, "rsec", "lsec"),
        P("lsec"),
        P("rsec"),
        P(),
    )
    out_specs = (P("lsec", "rsec"), P("lsec", "rsec"), P())
    return jax.shard_map(
        functools.partial(on_device, nl, nr),
        mesh=mesh, in_specs=in_specs, out_specs=out_specs, check_vma=False,
    )
```

```python
import functools

import jax
import jax.numpy as jnp
from jax import lax
from jax.experimental import pallas as pl
from jax.experimental.pallas import tpu as pltpu
from jax.sharding import PartitionSpec as P

MESH = pl.DeviceIdType.MESH
F32 = jnp.float32
BF16 = jnp.bfloat16
NT = (((1,), (1,)), ((), ()))
NN = (((1,), (0,)), ((), ()))


def kernel(
    nl, nr, gather_right, terms,
    shift_ref, ldim_ref, rdim_ref, psi_hbm, left_hbm, right_hbm,
    image1_ref, image2_ref, proj_ref,
    psi_ref, live, first, images, inner, lbuf, rbuf, w1_ref, part, row_sum, row_slots, col_slots,
    l_send, l_recv, r_send, r_recv, h_send, h_recv, ar_send, ar_recv, ac_send, ac_recv, own_sem,
):
    width = psi_hbm.shape[0]
    count = float(nl * nr * width * width)
    li, ri = lax.axis_index("lsec"), lax.axis_index("rsec")
    pending = []
    own = [
        pltpu.make_async_copy(psi_hbm, psi_ref, own_sem.at[0]),
        pltpu.make_async_copy(left_hbm, lbuf.at[ri], own_sem.at[1]),
        pltpu.make_async_copy(right_hbm, rbuf.at[li] if gather_right else rbuf, own_sem.at[2]),
    ]
    for copy in own:
        copy.start()

    def when(cond, fn):
        if cond is None:
            fn()
        else:
            pl.when(cond)(fn)

    def send(src, dst, send_sem, recv_sem, device, cond=None):
        copy = pltpu.make_async_remote_copy(
            src_ref=src, dst_ref=dst, send_sem=send_sem, recv_sem=recv_sem,
            device_id=device, device_id_type=MESH,
        )
        when(cond, copy.start)
        pending.append((copy, cond))

    def arrive(dst, send_sem, recv_sem, device, cond=None):
        copy = pltpu.make_async_remote_copy(
            src_ref=dst, dst_ref=dst, send_sem=send_sem, recv_sem=recv_sem,
            device_id=device, device_id_type=MESH,
        )
        when(cond, copy.wait_recv)

    def drain(n):
        for copy, cond in pending[:n]:
            when(cond, copy.wait_send)
        del pending[:n]

    barrier = pltpu.get_barrier_semaphore()

    def greet_col(i, _):
        pl.semaphore_signal(
            barrier, inc=1, device_id=(lax.rem(li + i, nl), ri), device_id_type=MESH
        )
        return 0

    def greet_row(i, _):
        pl.semaphore_signal(
            barrier, inc=1, device_id=(li, lax.rem(ri + i, nr)), device_id_type=MESH
        )
        return 0

    lax.fori_loop(1, nl, greet_col, 0)
    lax.fori_loop(1, nr, greet_row, 0)

    rows = lax.broadcasted_iota(jnp.int32, (width, width), 0)
    cols = lax.broadcasted_iota(jnp.int32, (width, width), 1)
    mask = ((rows < ldim_ref[0]) & (cols < rdim_ref[0])).astype(F32)

    def lanes(x):
        total = jnp.sum(x, axis=0, keepdims=True)
        out = total[:, 0:128]
        for at in range(128, width, 128):
            out = out + total[:, at:at + 128]
        return out

    own[0].wait()
    live32 = psi_ref[...].astype(F32) * mask
    live[4] = live32.astype(BF16)
    part[...] = jnp.zeros_like(part)
    part[0, 0:1, :] = lanes(live32 * live32)


    for store in (live, images):
        for k in range(9):
            dl, dr = k // 3 - 1, k % 3 - 1
            outside = (li - dl < 0) | (li - dl >= nl) | (ri - dr < 0) | (ri - dr >= nr)
            if k != 4:
                def clear(store=store, k=k):
                    store[k] = jnp.zeros((width, width), BF16)
                pl.when(outside)(clear)

    pl.semaphore_wait(barrier, nl + nr - 2)

    def reduce_start(t):
        for i in range(1, nr):
            other = lax.rem(ri + i, nr)
            send(part.at[t], row_slots.at[t, ri], ar_send.at[t, i], ar_recv.at[t, ri], (li, other))

    def reduce_middle(t):
        for i in range(1, nr):
            other = lax.rem(ri + i, nr)
            arrive(row_slots.at[t, other], ar_send.at[t, i], ar_recv.at[t, other], (li, other))
        row_slots[t, pl.ds(ri, 1)] = part[t][None]
        total = row_slots[t, 0]
        for i in range(1, nr):
            total = total + row_slots[t, i]
        row_sum[t] = total
        for i in range(1, nl):
            other = lax.rem(li + i, nl)
            send(row_sum.at[t], col_slots.at[t, li], ac_send.at[t, i], ac_recv.at[t, li], (other, ri))

    def reduce_end(t):
        for i in range(1, nl):
            other = lax.rem(li + i, nl)
            arrive(col_slots.at[t, other], ac_send.at[t, i], ac_recv.at[t, other], (other, ri))
        col_slots[t, pl.ds(li, 1)] = row_sum[t][None]
        total = col_slots[t, 0]
        for i in range(1, nl):
            total = total + col_slots[t, i]
        return jnp.sum(total, axis=1, keepdims=True)

    def gather(mine, buf, n, me, device, send_sem, recv_sem, parts, balance):
        outer = n // 2
        o, i = me // 2, lax.rem(me, 2)
        pair = me + 1 - 2 * i
        pair_dev = device(pair)
        balance = balance and parts == 2 and outer > 2 and outer % 2 == 0
        mate = o + 1 - 2 * lax.rem(o, 2)
        size = buf.shape[1] // parts

        def piece(at, h):
            return buf.at[at, pl.ds(h * size, size)]

        def put(at, h, sem, dev, cond, src=None):
            src = piece(at, h) if src is None else src
            send(src, piece(at, h), sem, recv_sem.at[h, at], dev, cond)

        def got(at, h, cond=None):
            arrive(piece(at, h), send_sem.at[2, h, 0], recv_sem.at[h, at], pair_dev, cond)

        def forward(slot, h, cond=None):
            if balance and h == 1:
                cond = (slot != mate) if cond is None else cond & (slot != mate)
            put(slot * 2 + i, h, send_sem.at[2, h, slot], pair_dev, cond)

        for s in range(outer - 1):
            low, high = o - s, o + s
            up = device(jnp.minimum(me + 2, n - 1))
            down = device(jnp.maximum(me - 2, 0))
            for h in range(parts):
                src = mine.at[pl.ds(h * size, size)] if s == 0 else None
                put(jnp.maximum(low, 0) * 2 + i, h, send_sem.at[0, h, s], up,
                    (low >= 0) & (o < outer - 1), src)
                put(jnp.minimum(high, outer - 1) * 2 + i, h, send_sem.at[1, h, s], down,
                    (high < outer) & (o > 0), src)
            if s == 0:
                for h in range(parts):
                    put(me, h, send_sem.at[2, h, o], pair_dev, None, mine.at[pl.ds(h * size, size)])
            if balance and s == 1:
                got(o * 2 + 1 - i, 1)
                put(o * 2 + 1 - i, 1, send_sem.at[3, 0, 0], device(mate * 2 + i), None)
            yield
            for h in range(parts):
                for slot, cond in ((low - 1, low - 1 >= 0), (high + 1, high + 1 < outer)):
                    slot = jnp.clip(slot, 0, outer - 1)
                    got(slot * 2 + i, h, cond)
                    forward(slot, h, cond)
        yield
        for slot in range(outer):
            for h in range(parts):
                early = balance and h == 1
                got(slot * 2 + 1 - i, h, (slot != o) if early else None)

    def halo(buf, t, chunks):
        outer = nl // 2
        o, i = li // 2, lax.rem(li, 2)
        from_pair, from_line = 1 + 6 * i, 7 - 6 * i
        pair = (li + 1 - 2 * i, ri)
        onward = (jnp.clip(li + 2 - 4 * i, 0, nl - 1), ri)
        goes = ((i == 0) & (o < outer - 1)) | ((i == 1) & (o > 0))
        comes = ((i == 0) & (o > 0)) | ((i == 1) & (o < outer - 1))
        east, west = (li, jnp.minimum(ri + 1, nr - 1)), (li, jnp.maximum(ri - 1, 0))
        size = width // chunks

        def piece(k, c):
            return buf.at[k, pl.ds(c * size, size)]

        def put(src, dst, c, sem, dev, cond=None):
            send(piece(src, c), piece(dst, c), h_send.at[t, c, sem], h_recv.at[t, c, dst], dev, cond)

        def got(k, c, cond=None):
            arrive(piece(k, c), h_send.at[t, c, k], h_recv.at[t, c, k], pair, cond)

        def sideways(k, c, cond):
            go = ri < nr - 1
            put(k, k + 1, c, k + 1, east, go if cond is None else go & cond)
            go = ri > 0
            put(k, k - 1, c, k - 1, west, go if cond is None else go & cond)

        for c in range(chunks):
            put(4, from_line, c, 4, pair)
            sideways(4, c, None)
            yield
        for c in range(chunks):
            got(from_pair, c)
            put(from_pair, from_line, c, from_pair, onward, goes)
            sideways(from_pair, c, None)
        yield
        for c in range(chunks):
            got(from_line, c, comes)
            sideways(from_line, c, comes)
        yield
        for c in range(chunks):
            for k, l_ok in ((4, None), (from_pair, None), (from_line, comes)):
                for at, r_ok in ((k + 1, ri > 0), (k - 1, ri < nr - 1)):
                    got(at, c, r_ok if l_ok is None else r_ok & l_ok)

    def apply_left(vec):
        def term(w, _):
            k = (shift_ref[0, w] + 1) * 3 + shift_ref[1, w] + 1
            product = jnp.dot(
                lbuf[:, w].reshape(width, width), vec[k], preferred_element_type=F32
            )
            inner[w] = product.astype(BF16)
            return 0

        lax.fori_loop(0, terms, term, 0, unroll=True)

    def apply_right(c):
        half = width
        at = slice(c * half, (c + 1) * half)

        def term(w, total):
            if gather_right:
                b, dims = rbuf[:, w].reshape(width, width), NT
            else:
                b, dims = rbuf[w], NN
            return total + lax.dot_general(inner[w, at], b, dims, preferred_element_type=F32)

        total = lax.fori_loop(0, terms, term, jnp.zeros((half, width), F32), unroll=True)
        return total * mask[at]

    reduce_start(0)
    left = gather(left_hbm, lbuf, nr, ri, lambda r: (li, r), l_send, l_recv, 1, False)
    right = iter(())
    if gather_right:
        right = gather(right_hbm, rbuf, nl, li, lambda l: (l, ri), r_send, r_recv, 1, False)
    halo1 = halo(live, 0, 1)
    next(right, None)
    next(halo1)
    next(left)
    next(right, None)
    next(halo1)
    reduce_middle(0)
    next(left, None)
    next(right, None)
    next(halo1)
    for _ in range(nl // 2 - 3):
        next(right, None)
    for _ in halo1:
        pass
    scale = lax.rsqrt(reduce_end(0)[0:1] / count + 1e-06)
    for k in range(9):
        first[k] = (live[k].astype(F32) * scale).astype(BF16)
    for _ in left:
        pass
    own[1].wait()
    apply_left(first)
    own[2].wait()
    for _ in right:
        pass
    half = width
    early = len(pending)
    halo2 = halo(images, 1, 1)
    for c in range(1):
        at = slice(c * half, (c + 1) * half)
        w1 = apply_right(c)
        w1_ref[at] = w1
        w1_bf16 = w1.astype(BF16)
        images[4, at] = w1_bf16
        next(halo2)
        image1_ref[at] = w1_bf16
    w1 = w1_ref[...]
    v1 = first[4].astype(F32)
    part[1, 0:1, :] = lanes(v1 * w1)
    part[1, 1:2, :] = lanes(w1 * w1)
    part[1, 2:3, :] = lanes(v1 * v1)
    reduce_start(1)
    next(halo2)
    reduce_middle(1)
    next(halo2)
    drain(early)
    for _ in halo2:
        pass
    apply_left(images)
    sums = reduce_end(1)
    alpha = sums[0:1] / count
    nr_ = sums[1:2] / count - 2.0 * alpha * alpha + alpha * alpha * (sums[2:3] / count)
    factor = lax.rsqrt(jnp.maximum(nr_, 0.0) + 1e-06)
    totals = [jnp.zeros((1, 128), F32)] * 3
    for c in range(1):
        at = slice(c * half, (c + 1) * half)
        w1 = w1_ref[at]
        w2 = (apply_right(c) - alpha * w1) * factor
        image2_ref[at] = w2.astype(BF16)
        v1 = first[4, at].astype(F32)
        v2 = ((w1 - alpha * v1) * factor).astype(BF16).astype(F32)
        products = (v1 * w2, v2 * w1, v2 * w2)
        totals = [total + lanes(product) for total, product in zip(totals, products)]
    for k in range(3):
        part[2, k:k + 1, :] = totals[k]
    reduce_start(2)
    reduce_middle(2)
    sums = reduce_end(2) / count
    r8 = lax.broadcasted_iota(jnp.int32, (8, 128), 0)
    c8 = lax.broadcasted_iota(jnp.int32, (8, 128), 1)
    top = jnp.where(c8 == 0, alpha, sums[0:1])
    bottom = jnp.where(c8 == 0, sums[1:2], sums[2:3])
    proj_ref[...] = jnp.where(r8 == 0, top, bottom)[:2, :2]

    drain(len(pending))


def on_device(nl, nr, psi, left_env, right_env, left_dims, right_dims, term_shift):
    width = psi.shape[0]
    terms = left_env.shape[0]
    mine = left_env.shape[1]
    ncol = right_env.shape[2]
    gather_right = ncol % 16 == 0
    if gather_right:
        right = jnp.swapaxes(right_env, 1, 2)
        rshape = (nl, terms, ncol, width)
    else:
        right = lax.all_gather(right_env, "lsec", axis=2, tiled=True)
        rshape = (terms, width, width)
    vmem = pl.BlockSpec(memory_space=pltpu.VMEM)
    hbm = pl.BlockSpec(memory_space=pltpu.HBM)
    smem = pl.BlockSpec(memory_space=pltpu.SMEM)
    dma = pltpu.SemaphoreType.DMA
    image1, image2, proj = pl.pallas_call(
        functools.partial(kernel, nl, nr, gather_right, terms),
        out_shape=(
            jax.ShapeDtypeStruct((width, width), BF16),
            jax.ShapeDtypeStruct((width, width), BF16),
            jax.ShapeDtypeStruct((2, 2), F32),
        ),
        in_specs=[smem] * 3 + [hbm] * 3,
        out_specs=(vmem, vmem, vmem),
        scratch_shapes=[
            pltpu.VMEM((width, width), BF16),
            pltpu.VMEM((9, width, width), BF16),
            pltpu.VMEM((9, width, width), BF16),
            pltpu.VMEM((9, width, width), BF16),
            pltpu.VMEM((terms, width, width), BF16),
            pltpu.VMEM((nr, terms, mine, width), BF16),
            pltpu.VMEM(rshape, BF16),
            pltpu.VMEM((width, width), F32),
            pltpu.VMEM((3, 8, 128), F32),
            pltpu.VMEM((3, 8, 128), F32),
            pltpu.VMEM((3, nr, 8, 128), F32),
            pltpu.VMEM((3, nl, 8, 128), F32),
            dma((3, 2, nr)),
            dma((2, nr)),
            dma((4, 2, nl)),
            dma((2, nl)),
            dma((2, 2, 9)),
            dma((2, 2, 9)),
            dma((3, nr)),
            dma((3, nr)),
            dma((3, nl)),
            dma((3, nl)),
            dma((3,)),
        ],
        compiler_params=pltpu.CompilerParams(
            collective_id=0, has_side_effects=True, vmem_limit_bytes=32 * 1024 * 1024
        ),
        cost_estimate=pl.CostEstimate(
            flops=8 * terms * width**3, bytes_accessed=4 * 2**20, transcendentals=2
        ),
    )(term_shift.T, left_dims, right_dims, psi, left_env, right)
    return image1, image2, proj


def solution(mesh):
    nl, nr = mesh.shape["lsec"], mesh.shape["rsec"]
    in_specs = (
        P("lsec", "rsec"),
        P(None, ("lsec", "rsec"), None),
        P(None, "rsec", "lsec"),
        P("lsec"),
        P("rsec"),
        P(),
    )
    out_specs = (P("lsec", "rsec"), P("lsec", "rsec"), P())
    return jax.shard_map(
        functools.partial(on_device, nl, nr),
        mesh=mesh, in_specs=in_specs, out_specs=out_specs, check_vma=False,
    )
```

```python
import functools

import jax
import jax.numpy as jnp
from jax import lax
from jax.experimental import pallas as pl
from jax.experimental.pallas import tpu as pltpu
from jax.sharding import PartitionSpec as P

MESH = pl.DeviceIdType.MESH
F32 = jnp.float32
BF16 = jnp.bfloat16
NT = (((1,), (1,)), ((), ()))
NN = (((1,), (0,)), ((), ()))


def kernel(
    nl, nr, gather_right, terms,
    shift_ref, ldim_ref, rdim_ref, psi_hbm, left_hbm, right_hbm,
    image1_hbm, image2_hbm, proj_ref,
    psi_ref, live, first, images, inner, lbuf, rbuf, w1_ref, part, row_sum, row_slots, col_slots,
    l_send, l_recv, r_send, r_recv, h_send, h_recv, ar_send, ar_recv, ac_send, ac_recv, own_sem,
):
    width = psi_hbm.shape[0]
    count = float(nl * nr * width * width)
    li, ri = lax.axis_index("lsec"), lax.axis_index("rsec")
    pending = []
    own = [
        pltpu.make_async_copy(psi_hbm, psi_ref, own_sem.at[0]),
        pltpu.make_async_copy(left_hbm, lbuf.at[ri], own_sem.at[1]),
        pltpu.make_async_copy(right_hbm, rbuf.at[li] if gather_right else rbuf, own_sem.at[2]),
    ]
    for copy in own:
        copy.start()

    def when(cond, fn):
        if cond is None:
            fn()
        else:
            pl.when(cond)(fn)

    def send(src, dst, send_sem, recv_sem, device, cond=None):
        copy = pltpu.make_async_remote_copy(
            src_ref=src, dst_ref=dst, send_sem=send_sem, recv_sem=recv_sem,
            device_id=device, device_id_type=MESH,
        )
        when(cond, copy.start)
        pending.append((copy, cond))

    def arrive(dst, send_sem, recv_sem, device, cond=None):
        copy = pltpu.make_async_remote_copy(
            src_ref=dst, dst_ref=dst, send_sem=send_sem, recv_sem=recv_sem,
            device_id=device, device_id_type=MESH,
        )
        when(cond, copy.wait_recv)

    def drain(n):
        for copy, cond in pending[:n]:
            when(cond, copy.wait_send)
        del pending[:n]

    barrier = pltpu.get_barrier_semaphore()

    def greet_col(i, _):
        pl.semaphore_signal(
            barrier, inc=1, device_id=(lax.rem(li + i, nl), ri), device_id_type=MESH
        )
        return 0

    def greet_row(i, _):
        pl.semaphore_signal(
            barrier, inc=1, device_id=(li, lax.rem(ri + i, nr)), device_id_type=MESH
        )
        return 0

    lax.fori_loop(1, nl, greet_col, 0)
    lax.fori_loop(1, nr, greet_row, 0)

    rows = lax.broadcasted_iota(jnp.int32, (width, width), 0)
    cols = lax.broadcasted_iota(jnp.int32, (width, width), 1)
    mask = ((rows < ldim_ref[0]) & (cols < rdim_ref[0])).astype(F32)

    def lanes(x):
        total = jnp.sum(x, axis=0, keepdims=True)
        out = total[:, 0:128]
        for at in range(128, width, 128):
            out = out + total[:, at:at + 128]
        return out

    own[0].wait()
    live32 = psi_ref[...].astype(F32) * mask
    live[4] = live32.astype(BF16)
    part[...] = jnp.zeros_like(part)
    part[0, 0:1, :] = lanes(live32 * live32)


    for store in (live, images):
        for k in range(9):
            dl, dr = k // 3 - 1, k % 3 - 1
            outside = (li - dl < 0) | (li - dl >= nl) | (ri - dr < 0) | (ri - dr >= nr)
            if k != 4:
                def clear(store=store, k=k):
                    store[k] = jnp.zeros((width, width), BF16)
                pl.when(outside)(clear)

    pl.semaphore_wait(barrier, nl + nr - 2)

    def reduce_start(t):
        for i in range(1, nr):
            other = lax.rem(ri + i, nr)
            send(part.at[t], row_slots.at[t, ri], ar_send.at[t, i], ar_recv.at[t, ri], (li, other))

    def reduce_middle(t):
        for i in range(1, nr):
            other = lax.rem(ri + i, nr)
            arrive(row_slots.at[t, other], ar_send.at[t, i], ar_recv.at[t, other], (li, other))
        row_slots[t, pl.ds(ri, 1)] = part[t][None]
        total = row_slots[t, 0]
        for i in range(1, nr):
            total = total + row_slots[t, i]
        row_sum[t] = total
        for i in range(1, nl):
            other = lax.rem(li + i, nl)
            send(row_sum.at[t], col_slots.at[t, li], ac_send.at[t, i], ac_recv.at[t, li], (other, ri))

    def reduce_end(t):
        for i in range(1, nl):
            other = lax.rem(li + i, nl)
            arrive(col_slots.at[t, other], ac_send.at[t, i], ac_recv.at[t, other], (other, ri))
        col_slots[t, pl.ds(li, 1)] = row_sum[t][None]
        total = col_slots[t, 0]
        for i in range(1, nl):
            total = total + col_slots[t, i]
        return jnp.sum(total, axis=1, keepdims=True)

    def gather(mine, buf, n, me, device, send_sem, recv_sem, parts, balance):
        outer = n // 2
        o, i = me // 2, lax.rem(me, 2)
        pair = me + 1 - 2 * i
        pair_dev = device(pair)
        balance = balance and parts == 2 and outer > 2 and outer % 2 == 0
        mate = o + 1 - 2 * lax.rem(o, 2)
        size = buf.shape[1] // parts

        def piece(at, h):
            return buf.at[at, pl.ds(h * size, size)]

        def put(at, h, sem, dev, cond, src=None):
            src = piece(at, h) if src is None else src
            send(src, piece(at, h), sem, recv_sem.at[h, at], dev, cond)

        def got(at, h, cond=None):
            arrive(piece(at, h), send_sem.at[2, h, 0], recv_sem.at[h, at], pair_dev, cond)

        def forward(slot, h, cond=None):
            if balance and h == 1:
                cond = (slot != mate) if cond is None else cond & (slot != mate)
            put(slot * 2 + i, h, send_sem.at[2, h, slot], pair_dev, cond)

        for s in range(outer - 1):
            low, high = o - s, o + s
            up = device(jnp.minimum(me + 2, n - 1))
            down = device(jnp.maximum(me - 2, 0))
            for h in range(parts):
                src = mine.at[pl.ds(h * size, size)] if s == 0 else None
                put(jnp.maximum(low, 0) * 2 + i, h, send_sem.at[0, h, s], up,
                    (low >= 0) & (o < outer - 1), src)
                put(jnp.minimum(high, outer - 1) * 2 + i, h, send_sem.at[1, h, s], down,
                    (high < outer) & (o > 0), src)
            if s == 0:
                for h in range(parts):
                    put(me, h, send_sem.at[2, h, o], pair_dev, None, mine.at[pl.ds(h * size, size)])
            if balance and s == 1:
                got(o * 2 + 1 - i, 1)
                put(o * 2 + 1 - i, 1, send_sem.at[3, 0, 0], device(mate * 2 + i), None)
            yield
            for h in range(parts):
                for slot, cond in ((low - 1, low - 1 >= 0), (high + 1, high + 1 < outer)):
                    slot = jnp.clip(slot, 0, outer - 1)
                    got(slot * 2 + i, h, cond)
                    forward(slot, h, cond)
        yield
        for slot in range(outer):
            for h in range(parts):
                early = balance and h == 1
                got(slot * 2 + 1 - i, h, (slot != o) if early else None)

    def halo(buf, t, chunks):
        outer = nl // 2
        o, i = li // 2, lax.rem(li, 2)
        from_pair, from_line = 1 + 6 * i, 7 - 6 * i
        pair = (li + 1 - 2 * i, ri)
        onward = (jnp.clip(li + 2 - 4 * i, 0, nl - 1), ri)
        goes = ((i == 0) & (o < outer - 1)) | ((i == 1) & (o > 0))
        comes = ((i == 0) & (o > 0)) | ((i == 1) & (o < outer - 1))
        east, west = (li, jnp.minimum(ri + 1, nr - 1)), (li, jnp.maximum(ri - 1, 0))
        size = width // chunks

        def piece(k, c):
            return buf.at[k, pl.ds(c * size, size)]

        def put(src, dst, c, sem, dev, cond=None):
            send(piece(src, c), piece(dst, c), h_send.at[t, c, sem], h_recv.at[t, c, dst], dev, cond)

        def got(k, c, cond=None):
            arrive(piece(k, c), h_send.at[t, c, k], h_recv.at[t, c, k], pair, cond)

        def sideways(k, c, cond):
            go = ri < nr - 1
            put(k, k + 1, c, k + 1, east, go if cond is None else go & cond)
            go = ri > 0
            put(k, k - 1, c, k - 1, west, go if cond is None else go & cond)

        for c in range(chunks):
            put(4, from_line, c, 4, pair)
            sideways(4, c, None)
            yield
        for c in range(chunks):
            got(from_pair, c)
            put(from_pair, from_line, c, from_pair, onward, goes)
            sideways(from_pair, c, None)
        yield
        for c in range(chunks):
            got(from_line, c, comes)
            sideways(from_line, c, comes)
        yield
        for c in range(chunks):
            for k, l_ok in ((4, None), (from_pair, None), (from_line, comes)):
                for at, r_ok in ((k + 1, ri > 0), (k - 1, ri < nr - 1)):
                    got(at, c, r_ok if l_ok is None else r_ok & l_ok)

    def apply_left(vec):
        def term(w, _):
            k = (shift_ref[0, w] + 1) * 3 + shift_ref[1, w] + 1
            product = jnp.dot(
                lbuf[:, w].reshape(width, width), vec[k], preferred_element_type=F32
            )
            inner[w] = product.astype(BF16)
            return 0

        lax.fori_loop(0, terms, term, 0, unroll=True)

    def apply_right(c):
        half = width
        at = slice(c * half, (c + 1) * half)

        def term(w, total):
            if gather_right:
                b, dims = rbuf[:, w].reshape(width, width), NT
            else:
                b, dims = rbuf[w], NN
            return total + lax.dot_general(inner[w, at], b, dims, preferred_element_type=F32)

        total = lax.fori_loop(0, terms, term, jnp.zeros((half, width), F32), unroll=True)
        return total * mask[at]

    reduce_start(0)
    left = gather(left_hbm, lbuf, nr, ri, lambda r: (li, r), l_send, l_recv, 1, False)
    right = iter(())
    if gather_right:
        right = gather(right_hbm, rbuf, nl, li, lambda l: (l, ri), r_send, r_recv, 1, False)
    halo1 = halo(live, 0, 1)
    next(right, None)
    next(halo1)
    next(left)
    next(right, None)
    next(halo1)
    reduce_middle(0)
    next(left, None)
    next(right, None)
    next(halo1)
    for _ in range(nl // 2 - 3):
        next(right, None)
    for _ in halo1:
        pass
    scale = lax.rsqrt(reduce_end(0)[0:1] / count + 1e-06)
    for k in range(9):
        first[k] = (live[k].astype(F32) * scale).astype(BF16)
    for _ in left:
        pass
    own[1].wait()
    apply_left(first)
    own[2].wait()
    for _ in right:
        pass
    half = width
    early = len(pending)
    halo2 = halo(images, 1, 1)
    for c in range(1):
        at = slice(c * half, (c + 1) * half)
        w1 = apply_right(c)
        w1_ref[at] = w1
        w1_bf16 = w1.astype(BF16)
        images[4, at] = w1_bf16
        next(halo2)
    image1_out = pltpu.make_async_copy(images.at[4], image1_hbm, own_sem.at[3])
    image1_out.start()
    w1 = w1_ref[...]
    v1 = first[4].astype(F32)
    part[1, 0:1, :] = lanes(v1 * w1)
    part[1, 1:2, :] = lanes(w1 * w1)
    part[1, 2:3, :] = lanes(v1 * v1)
    reduce_start(1)
    next(halo2)
    reduce_middle(1)
    next(halo2)
    drain(early)
    for _ in halo2:
        pass
    apply_left(images)
    sums = reduce_end(1)
    alpha = sums[0:1] / count
    nr_ = sums[1:2] / count - 2.0 * alpha * alpha + alpha * alpha * (sums[2:3] / count)
    factor = lax.rsqrt(jnp.maximum(nr_, 0.0) + 1e-06)
    totals = [jnp.zeros((1, 128), F32)] * 3
    for c in range(1):
        at = slice(c * half, (c + 1) * half)
        w1 = w1_ref[at]
        w2 = (apply_right(c) - alpha * w1) * factor
        psi_ref[at] = w2.astype(BF16)
        v1 = first[4, at].astype(F32)
        v2 = ((w1 - alpha * v1) * factor).astype(BF16).astype(F32)
        products = (v1 * w2, v2 * w1, v2 * w2)
        totals = [total + lanes(product) for total, product in zip(totals, products)]
    for k in range(3):
        part[2, k:k + 1, :] = totals[k]
    reduce_start(2)
    image2_out = pltpu.make_async_copy(psi_ref, image2_hbm, own_sem.at[4])
    image2_out.start()
    reduce_middle(2)
    sums = reduce_end(2) / count
    r8 = lax.broadcasted_iota(jnp.int32, (8, 128), 0)
    c8 = lax.broadcasted_iota(jnp.int32, (8, 128), 1)
    top = jnp.where(c8 == 0, alpha, sums[0:1])
    bottom = jnp.where(c8 == 0, sums[1:2], sums[2:3])
    proj_ref[...] = jnp.where(r8 == 0, top, bottom)[:2, :2]

    image1_out.wait()
    image2_out.wait()
    drain(len(pending))


def on_device(nl, nr, psi, left_env, right_env, left_dims, right_dims, term_shift):
    width = psi.shape[0]
    terms = left_env.shape[0]
    mine = left_env.shape[1]
    ncol = right_env.shape[2]
    gather_right = ncol % 16 == 0
    if gather_right:
        right = jnp.swapaxes(right_env, 1, 2)
        rshape = (nl, terms, ncol, width)
    else:
        right = lax.all_gather(right_env, "lsec", axis=2, tiled=True)
        rshape = (terms, width, width)
    vmem = pl.BlockSpec(memory_space=pltpu.VMEM)
    hbm = pl.BlockSpec(memory_space=pl.ANY)
    smem = pl.BlockSpec(memory_space=pltpu.SMEM)
    dma = pltpu.SemaphoreType.DMA
    image1, image2, proj = pl.pallas_call(
        functools.partial(kernel, nl, nr, gather_right, terms),
        out_shape=(
            jax.ShapeDtypeStruct((width, width), BF16),
            jax.ShapeDtypeStruct((width, width), BF16),
            jax.ShapeDtypeStruct((2, 2), F32),
        ),
        in_specs=[smem] * 3 + [hbm] * 3,
        out_specs=(hbm, hbm, vmem),
        scratch_shapes=[
            pltpu.VMEM((width, width), BF16),
            pltpu.VMEM((9, width, width), BF16),
            pltpu.VMEM((9, width, width), BF16),
            pltpu.VMEM((9, width, width), BF16),
            pltpu.VMEM((terms, width, width), BF16),
            pltpu.VMEM((nr, terms, mine, width), BF16),
            pltpu.VMEM(rshape, BF16),
            pltpu.VMEM((width, width), F32),
            pltpu.VMEM((3, 8, 128), F32),
            pltpu.VMEM((3, 8, 128), F32),
            pltpu.VMEM((3, nr, 8, 128), F32),
            pltpu.VMEM((3, nl, 8, 128), F32),
            dma((3, 2, nr)),
            dma((2, nr)),
            dma((4, 2, nl)),
            dma((2, nl)),
            dma((2, 2, 9)),
            dma((2, 2, 9)),
            dma((3, nr)),
            dma((3, nr)),
            dma((3, nl)),
            dma((3, nl)),
            dma((5,)),
        ],
        compiler_params=pltpu.CompilerParams(
            collective_id=0, has_side_effects=True, vmem_limit_bytes=56 * 1024 * 1024
        ),
        cost_estimate=pl.CostEstimate(
            flops=8 * terms * width**3, bytes_accessed=4 * 2**20, transcendentals=2
        ),
    )(term_shift.T, left_dims, right_dims, psi, left_env, right)
    return image1, image2, proj


def solution(mesh):
    nl, nr = mesh.shape["lsec"], mesh.shape["rsec"]
    in_specs = (
        P("lsec", "rsec"),
        P(None, ("lsec", "rsec"), None),
        P(None, "rsec", "lsec"),
        P("lsec"),
        P("rsec"),
        P(),
    )
    out_specs = (P("lsec", "rsec"), P("lsec", "rsec"), P())
    return jax.shard_map(
        functools.partial(on_device, nl, nr),
        mesh=mesh, in_specs=in_specs, out_specs=out_specs, check_vma=False,
    )
```

```python
import functools

import jax
import jax.numpy as jnp
from jax import lax
from jax.experimental import pallas as pl
from jax.experimental.pallas import tpu as pltpu
from jax.sharding import PartitionSpec as P

MESH = pl.DeviceIdType.MESH
F32 = jnp.float32
BF16 = jnp.bfloat16
NT = (((1,), (1,)), ((), ()))
NN = (((1,), (0,)), ((), ()))


def kernel(
    nl, nr, gather_right, terms,
    shift_ref, ldim_ref, rdim_ref, psi_hbm, left_hbm, right_hbm,
    image1_hbm, image2_hbm, proj_ref,
    psi_ref, live, first, images, inner, lbuf, rbuf, w1_ref, part, row_sum, row_slots, col_slots,
    l_send, l_recv, r_send, r_recv, h_send, h_recv, ar_send, ar_recv, ac_send, ac_recv, own_sem,
):
    width = psi_hbm.shape[0]
    count = float(nl * nr * width * width)
    li, ri = lax.axis_index("lsec"), lax.axis_index("rsec")
    pending = []
    own = [
        pltpu.make_async_copy(psi_hbm, psi_ref, own_sem.at[0]),
        pltpu.make_async_copy(left_hbm, lbuf.at[ri], own_sem.at[1]),
        pltpu.make_async_copy(right_hbm, rbuf.at[li] if gather_right else rbuf, own_sem.at[2]),
    ]
    for copy in own:
        copy.start()

    def when(cond, fn):
        if cond is None:
            fn()
        else:
            pl.when(cond)(fn)

    def send(src, dst, send_sem, recv_sem, device, cond=None):
        copy = pltpu.make_async_remote_copy(
            src_ref=src, dst_ref=dst, send_sem=send_sem, recv_sem=recv_sem,
            device_id=device, device_id_type=MESH,
        )
        when(cond, copy.start)
        pending.append((copy, cond))

    def arrive(dst, send_sem, recv_sem, device, cond=None):
        copy = pltpu.make_async_remote_copy(
            src_ref=dst, dst_ref=dst, send_sem=send_sem, recv_sem=recv_sem,
            device_id=device, device_id_type=MESH,
        )
        when(cond, copy.wait_recv)

    def drain(n):
        for copy, cond in pending[:n]:
            when(cond, copy.wait_send)
        del pending[:n]

    barrier = pltpu.get_barrier_semaphore()

    def greet_col(i, _):
        pl.semaphore_signal(
            barrier, inc=1, device_id=(lax.rem(li + i, nl), ri), device_id_type=MESH
        )
        return 0

    def greet_row(i, _):
        pl.semaphore_signal(
            barrier, inc=1, device_id=(li, lax.rem(ri + i, nr)), device_id_type=MESH
        )
        return 0

    lax.fori_loop(1, nl, greet_col, 0)
    lax.fori_loop(1, nr, greet_row, 0)

    rows = lax.broadcasted_iota(jnp.int32, (width, width), 0)
    cols = lax.broadcasted_iota(jnp.int32, (width, width), 1)
    mask = ((rows < ldim_ref[0]) & (cols < rdim_ref[0])).astype(F32)

    def lanes(x):
        total = jnp.sum(x, axis=0, keepdims=True)
        out = total[:, 0:128]
        for at in range(128, width, 128):
            out = out + total[:, at:at + 128]
        return out

    own[0].wait()
    live32 = psi_ref[...].astype(F32) * mask
    live[4] = live32.astype(BF16)
    part[...] = jnp.zeros_like(part)
    part[0, 0:1, :] = lanes(live32 * live32)


    for store in (live, images):
        for k in range(9):
            dl, dr = k // 3 - 1, k % 3 - 1
            outside = (li - dl < 0) | (li - dl >= nl) | (ri - dr < 0) | (ri - dr >= nr)
            if k != 4:
                def clear(store=store, k=k):
                    store[k] = jnp.zeros((width, width), BF16)
                pl.when(outside)(clear)

    pl.semaphore_wait(barrier, nl + nr - 2)

    def reduce_start(t):
        for i in range(1, nr):
            other = lax.rem(ri + i, nr)
            send(part.at[t], row_slots.at[t, ri], ar_send.at[t, i], ar_recv.at[t, ri], (li, other))

    def reduce_middle(t):
        for i in range(1, nr):
            other = lax.rem(ri + i, nr)
            arrive(row_slots.at[t, other], ar_send.at[t, i], ar_recv.at[t, other], (li, other))
        row_slots[t, pl.ds(ri, 1)] = part[t][None]
        total = row_slots[t, 0]
        for i in range(1, nr):
            total = total + row_slots[t, i]
        row_sum[t] = total
        for i in range(1, nl):
            other = lax.rem(li + i, nl)
            send(row_sum.at[t], col_slots.at[t, li], ac_send.at[t, i], ac_recv.at[t, li], (other, ri))

    def reduce_end(t):
        for i in range(1, nl):
            other = lax.rem(li + i, nl)
            arrive(col_slots.at[t, other], ac_send.at[t, i], ac_recv.at[t, other], (other, ri))
        col_slots[t, pl.ds(li, 1)] = row_sum[t][None]
        total = col_slots[t, 0]
        for i in range(1, nl):
            total = total + col_slots[t, i]
        return jnp.sum(total, axis=1, keepdims=True)

    def gather(mine, buf, n, me, device, send_sem, recv_sem, parts, balance):
        outer = n // 2
        o, i = me // 2, lax.rem(me, 2)
        pair = me + 1 - 2 * i
        pair_dev = device(pair)
        balance = balance and parts == 2 and outer > 2 and outer % 2 == 0
        mate = o + 1 - 2 * lax.rem(o, 2)
        size = buf.shape[1] // parts

        def piece(at, h):
            return buf.at[at, pl.ds(h * size, size)]

        def put(at, h, sem, dev, cond, src=None):
            src = piece(at, h) if src is None else src
            send(src, piece(at, h), sem, recv_sem.at[h, at], dev, cond)

        def got(at, h, cond=None):
            arrive(piece(at, h), send_sem.at[2, h, 0], recv_sem.at[h, at], pair_dev, cond)

        def forward(slot, h, cond=None):
            if balance and h == 1:
                cond = (slot != mate) if cond is None else cond & (slot != mate)
            put(slot * 2 + i, h, send_sem.at[2, h, slot], pair_dev, cond)

        for s in range(outer - 1):
            low, high = o - s, o + s
            up = device(jnp.minimum(me + 2, n - 1))
            down = device(jnp.maximum(me - 2, 0))
            for h in range(parts):
                src = mine.at[pl.ds(h * size, size)] if s == 0 else None
                put(jnp.maximum(low, 0) * 2 + i, h, send_sem.at[0, h, s], up,
                    (low >= 0) & (o < outer - 1), src)
                put(jnp.minimum(high, outer - 1) * 2 + i, h, send_sem.at[1, h, s], down,
                    (high < outer) & (o > 0), src)
            if s == 0:
                for h in range(parts):
                    put(me, h, send_sem.at[2, h, o], pair_dev, None, mine.at[pl.ds(h * size, size)])
            if balance and s == 1:
                got(o * 2 + 1 - i, 1)
                put(o * 2 + 1 - i, 1, send_sem.at[3, 0, 0], device(mate * 2 + i), None)
            yield
            for h in range(parts):
                for slot, cond in ((low - 1, low - 1 >= 0), (high + 1, high + 1 < outer)):
                    slot = jnp.clip(slot, 0, outer - 1)
                    got(slot * 2 + i, h, cond)
                    forward(slot, h, cond)
        yield
        for slot in range(outer):
            for h in range(parts):
                early = balance and h == 1
                got(slot * 2 + 1 - i, h, (slot != o) if early else None)

    def halo(buf, t, chunks):
        outer = nl // 2
        o, i = li // 2, lax.rem(li, 2)
        from_pair, from_line = 1 + 6 * i, 7 - 6 * i
        pair = (li + 1 - 2 * i, ri)
        onward = (jnp.clip(li + 2 - 4 * i, 0, nl - 1), ri)
        goes = ((i == 0) & (o < outer - 1)) | ((i == 1) & (o > 0))
        comes = ((i == 0) & (o > 0)) | ((i == 1) & (o < outer - 1))
        east, west = (li, jnp.minimum(ri + 1, nr - 1)), (li, jnp.maximum(ri - 1, 0))
        size = width // chunks

        def piece(k, c):
            return buf.at[k, pl.ds(c * size, size)]

        def put(src, dst, c, sem, dev, cond=None):
            send(piece(src, c), piece(dst, c), h_send.at[t, c, sem], h_recv.at[t, c, dst], dev, cond)

        def got(k, c, cond=None):
            arrive(piece(k, c), h_send.at[t, c, k], h_recv.at[t, c, k], pair, cond)

        def sideways(k, c, cond):
            go = ri < nr - 1
            put(k, k + 1, c, k + 1, east, go if cond is None else go & cond)
            go = ri > 0
            put(k, k - 1, c, k - 1, west, go if cond is None else go & cond)

        for c in range(chunks):
            put(4, from_line, c, 4, pair)
            sideways(4, c, None)
            yield
        for c in range(chunks):
            got(from_pair, c)
            put(from_pair, from_line, c, from_pair, onward, goes)
            sideways(from_pair, c, None)
        yield
        for c in range(chunks):
            got(from_line, c, comes)
            sideways(from_line, c, comes)
        yield
        for c in range(chunks):
            for k, l_ok in ((4, None), (from_pair, None), (from_line, comes)):
                for at, r_ok in ((k + 1, ri > 0), (k - 1, ri < nr - 1)):
                    got(at, c, r_ok if l_ok is None else r_ok & l_ok)

    def apply_left(vec):
        def term(w, _):
            k = (shift_ref[0, w] + 1) * 3 + shift_ref[1, w] + 1
            product = jnp.dot(
                lbuf[:, w].reshape(width, width), vec[k], preferred_element_type=F32
            )
            inner[w] = product.astype(BF16)
            return 0

        lax.fori_loop(0, terms, term, 0, unroll=True)

    def apply_right(c):
        half = width
        at = slice(c * half, (c + 1) * half)

        def term(w, total):
            if gather_right:
                b, dims = rbuf[:, w].reshape(width, width), NT
            else:
                b, dims = rbuf[w], NN
            return total + lax.dot_general(inner[w, at], b, dims, preferred_element_type=F32)

        total = lax.fori_loop(0, terms, term, jnp.zeros((half, width), F32), unroll=True)
        return total * mask[at]

    reduce_start(0)
    left = gather(left_hbm, lbuf, nr, ri, lambda r: (li, r), l_send, l_recv, 1, False)
    right = iter(())
    if gather_right:
        right = gather(right_hbm, rbuf, nl, li, lambda l: (l, ri), r_send, r_recv, 1, False)
    halo1 = halo(live, 0, 1)
    next(right, None)
    next(halo1)
    next(left)
    next(right, None)
    next(halo1)
    reduce_middle(0)
    next(left, None)
    next(right, None)
    next(halo1)
    for _ in range(nl // 2 - 3):
        next(right, None)
    for _ in halo1:
        pass
    scale = lax.rsqrt(reduce_end(0)[0:1] / count + 1e-06)
    for k in range(9):
        first[k] = (live[k].astype(F32) * scale).astype(BF16)
    for _ in left:
        pass
    own[1].wait()
    apply_left(first)
    own[2].wait()
    for _ in right:
        pass
    half = width
    early = len(pending)
    halo2 = halo(images, 1, 1)
    for c in range(1):
        at = slice(c * half, (c + 1) * half)
        w1 = apply_right(c)
        w1_ref[at] = w1
        w1_bf16 = w1.astype(BF16)
        images[4, at] = w1_bf16
        next(halo2)
    image1_out = pltpu.make_async_copy(images.at[4], image1_hbm, own_sem.at[3])
    image1_out.start()
    w1 = w1_ref[...]
    v1 = first[4].astype(F32)
    part[1, 0:1, :] = lanes(v1 * w1)
    part[1, 1:2, :] = lanes(w1 * w1)
    part[1, 2:3, :] = lanes(v1 * v1)
    reduce_start(1)
    next(halo2)
    reduce_middle(1)
    next(halo2)
    drain(early)
    for _ in halo2:
        pass
    apply_left(images)
    sums = reduce_end(1)
    alpha = sums[0:1] / count
    nr_ = sums[1:2] / count - 2.0 * alpha * alpha + alpha * alpha * (sums[2:3] / count)
    factor = lax.rsqrt(jnp.maximum(nr_, 0.0) + 1e-06)
    totals = [jnp.zeros((1, 128), F32)] * 3
    for c in range(1):
        at = slice(c * half, (c + 1) * half)
        w1 = w1_ref[at]
        w2 = (apply_right(c) - alpha * w1) * factor
        psi_ref[at] = w2.astype(BF16)
        v1 = first[4, at].astype(F32)
        v2 = ((w1 - alpha * v1) * factor).astype(BF16).astype(F32)
        products = (v1 * w2, v2 * w1, v2 * w2)
        totals = [total + lanes(product) for total, product in zip(totals, products)]
    for k in range(3):
        part[2, k:k + 1, :] = totals[k]
    late = len(pending)
    reduce_start(2)
    image2_out = pltpu.make_async_copy(psi_ref, image2_hbm, own_sem.at[4])
    image2_out.start()
    drain(late)
    image1_out.wait()
    reduce_middle(2)
    sums = reduce_end(2) / count
    r8 = lax.broadcasted_iota(jnp.int32, (8, 128), 0)
    c8 = lax.broadcasted_iota(jnp.int32, (8, 128), 1)
    top = jnp.where(c8 == 0, alpha, sums[0:1])
    bottom = jnp.where(c8 == 0, sums[1:2], sums[2:3])
    proj_ref[...] = jnp.where(r8 == 0, top, bottom)[:2, :2]

    image2_out.wait()
    drain(len(pending))


def on_device(nl, nr, psi, left_env, right_env, left_dims, right_dims, term_shift):
    width = psi.shape[0]
    terms = left_env.shape[0]
    mine = left_env.shape[1]
    ncol = right_env.shape[2]
    gather_right = ncol % 16 == 0
    if gather_right:
        right = jnp.swapaxes(right_env, 1, 2)
        rshape = (nl, terms, ncol, width)
    else:
        right = lax.all_gather(right_env, "lsec", axis=2, tiled=True)
        rshape = (terms, width, width)
    vmem = pl.BlockSpec(memory_space=pltpu.VMEM)
    hbm = pl.BlockSpec(memory_space=pl.ANY)
    smem = pl.BlockSpec(memory_space=pltpu.SMEM)
    dma = pltpu.SemaphoreType.DMA
    image1, image2, proj = pl.pallas_call(
        functools.partial(kernel, nl, nr, gather_right, terms),
        out_shape=(
            jax.ShapeDtypeStruct((width, width), BF16),
            jax.ShapeDtypeStruct((width, width), BF16),
            jax.ShapeDtypeStruct((2, 2), F32),
        ),
        in_specs=[smem] * 3 + [hbm] * 3,
        out_specs=(hbm, hbm, vmem),
        scratch_shapes=[
            pltpu.VMEM((width, width), BF16),
            pltpu.VMEM((9, width, width), BF16),
            pltpu.VMEM((9, width, width), BF16),
            pltpu.VMEM((9, width, width), BF16),
            pltpu.VMEM((terms, width, width), BF16),
            pltpu.VMEM((nr, terms, mine, width), BF16),
            pltpu.VMEM(rshape, BF16),
            pltpu.VMEM((width, width), F32),
            pltpu.VMEM((3, 8, 128), F32),
            pltpu.VMEM((3, 8, 128), F32),
            pltpu.VMEM((3, nr, 8, 128), F32),
            pltpu.VMEM((3, nl, 8, 128), F32),
            dma((3, 2, nr)),
            dma((2, nr)),
            dma((4, 2, nl)),
            dma((2, nl)),
            dma((2, 2, 9)),
            dma((2, 2, 9)),
            dma((3, nr)),
            dma((3, nr)),
            dma((3, nl)),
            dma((3, nl)),
            dma((5,)),
        ],
        compiler_params=pltpu.CompilerParams(
            collective_id=0, has_side_effects=True, vmem_limit_bytes=56 * 1024 * 1024
        ),
        cost_estimate=pl.CostEstimate(
            flops=8 * terms * width**3, bytes_accessed=4 * 2**20, transcendentals=2
        ),
    )(term_shift.T, left_dims, right_dims, psi, left_env, right)
    return image1, image2, proj


def solution(mesh):
    nl, nr = mesh.shape["lsec"], mesh.shape["rsec"]
    in_specs = (
        P("lsec", "rsec"),
        P(None, ("lsec", "rsec"), None),
        P(None, "rsec", "lsec"),
        P("lsec"),
        P("rsec"),
        P(),
    )
    out_specs = (P("lsec", "rsec"), P("lsec", "rsec"), P())
    return jax.shard_map(
        functools.partial(on_device, nl, nr),
        mesh=mesh, in_specs=in_specs, out_specs=out_specs, check_vma=False,
    )
```
